512 devices in a mesh: expert: 128 (over z, y, core), hidden: 4 (over x).
Axes of the slice: x: 4, y: 8, z: 8, core: 2. Of those that a mesh axis runs over, the one named last changes fastest.
Arguments:
- tokens: bfloat16 [16384, 4096], P('expert'), may hold values from -6 to 6
- enc_weight: bfloat16 [4096, 1024], P('expert', 'hidden'), may hold values from -0.09375 to 0.09375
- routes: int32 [16384, 8], P('expert'), may hold values from 0 to 127, all different within a row; in each aligned block of 128 rows (0 to 127, 128 to 255, ...) at most 16 rows name the same one
- gates: float32 [16384, 8], P('expert'), may hold values from 0.1 to 1
- gate_weight: bfloat16 [128, 1024, 1536], P('expert', None, 'hidden'), may hold values from -0.1875 to 0.1875
- up_weight: bfloat16 [128, 1024, 1536], P('expert', None, 'hidden'), may hold values from -0.1875 to 0.1875
- down_weight: bfloat16 [128, 1536, 1024], P('expert', None, 'hidden'), may hold values from -0.15625 to 0.15625
- dec_weight: bfloat16 [1024, 4096], P('expert', 'hidden'), may hold values from -0.1875 to 0.1875
Outputs:
- mixed: bfloat16 [16384, 4096], P('expert', 'hidden')
The draws below stay inside these ranges and needn't reach their ends.
Inputs may be any that keep to these rules, and one draw needn't show every extreme that they name: `routes`: each row names 8 different experts; within one group of 128 consecutive tokens no expert is named more than 16 times.
All inputs are finite; a program needn't handle non-finite values.
Results may differ from the reference program's by a relative error of at most 0.0076.
Values may be sent and summed in bfloat16 or wider, within the bound.
No kernel may reach another device: no remote copies, remote signals or barrier semaphores. Data moves between devices by JAX's collectives and lax.ppermute only.
A program may use at most 64 MiB of HBM per device.

```python
import math
import jax
import jax.numpy as jnp
import numpy as np
from jax import lax

D = 4096
LATENT = 1024
FF = 1536
TOP = 8
TOK_DEV = 128
EXPERTS = 128
TOKENS = 16384
CAP = 16
N_EXPERT = 128


def steps_of(rng, shape, split, smallest, largest):
    gain = 1.0
    for axis_at, parts in split:
        heights = jax.random.uniform(jax.random.fold_in(jax.random.fold_in(rng, 6), axis_at), (parts,), jnp.float32, smallest / len(split), largest / len(split))
        gain = gain * jnp.repeat(jnp.exp(heights), shape[axis_at] // parts).reshape((-1,) + (1,) * (len(shape) - 1 - axis_at))
    return gain


def assign_block(stream_key, own, number, rows, number_of, top, reach, slope):
    ranking = jax.random.permutation(stream_key, number_of)
    crowded, ordinary = portions_of(number_of, rows * top, reach, slope, True), portions_of(number_of, rows * top, reach, slope, False)
    places = jnp.arange(number_of)

    def named(lengths, turn):
        used = int((lengths > 0).sum())
        fixed = max(1, used // 4)
        moved = fixed + (places - fixed + turn * (used - fixed)) % max(1, number_of - fixed)
        return jnp.zeros((number_of,), jnp.int32).at[ranking[jnp.where(places < fixed, places, moved)]].set(jnp.asarray(lengths, jnp.int32))

    lengths = jnp.where(number % 4 == 0, named(crowded, number // 4), named(ordinary, number - number // 4 - 1))
    mixed = jax.random.permutation(jax.random.fold_in(own, 3), number_of)
    source_of, sink = mixed[0:number_of // 2 * 2:2], mixed[1:number_of // 2 * 2:2]
    room = jnp.minimum(lengths[source_of] - 1, reach - lengths[sink]) // 2
    room = jnp.where((source_of == ranking[0]) | (sink == ranking[0]) | (lengths[sink] == 0), 0, jnp.maximum(room, 0))
    moved = jax.random.randint(jax.random.fold_in(own, 4), (number_of // 2,), 0, 1 << 20) % (room + 1)
    lengths = lengths.at[source_of].add(-moved).at[sink].add(moved)
    items = jnp.searchsorted(jnp.cumsum(lengths), jnp.arange(rows * top), side="right").astype(jnp.int32)
    listing = items.reshape(top, rows).T
    listing = listing[jax.random.permutation(jax.random.fold_in(own, 1), rows)]
    turn = jax.random.randint(jax.random.fold_in(own, 2), (rows, 1), 0, top)
    return jnp.take_along_axis(listing, (jnp.arange(top)[None, :] + turn) % top, axis=1)


def portions_of(count, total, limit, skew, full):
    portions = [(1 << 20) // math.isqrt(grade ** skew) + 1 for grade in range(1, count + 1)]
    largest = limit if full else min(limit, max(-(-total // count), total * portions[0] // sum(portions)))
    least = 1 if total - largest >= count - 1 else 0
    counts, spare = [largest] + [least] * (count - 1), total - largest - least * (count - 1)
    while spare > 0:
        movable = [i for i in range(1, count) if counts[i] < largest] or [i for i in range(1, count) if counts[i] < limit]
        pool, budget = sum([portions[i] for i in movable]), spare
        for i in movable:
            addition = min(limit - counts[i], max(1, budget * portions[i] // pool), spare)
            counts[i] = counts[i] + addition
            spare = spare - addition
    return np.array(counts)


def normal_values(own_key, dims, deviation, limit, cuts=(), kind=jnp.bfloat16):
    loudness = steps_of(own_key, dims, cuts, -0.22, 0.18) if cuts else 1.0
    drawn = jax.random.normal(own_key, dims, jnp.float32) * deviation * loudness
    return jnp.minimum(jnp.maximum(drawn, -limit), limit).astype(kind)


def setup_inputs(seed: int = 0) -> dict:
    streams_of = jax.random.split(jax.random.key(seed), 9)
    tokens = normal_values(streams_of[0], (TOKENS, D), 1.0, 6.0, ((0, 128),))
    enc_weight = normal_values(streams_of[1], (D, LATENT), D ** -0.5, 0.09375, ((0, 128), (1, 4)))
    routes_keys = jax.random.split(jax.random.fold_in(streams_of[2], 1), TOKENS // TOK_DEV)
    routes_turns = jax.random.permutation(jax.random.fold_in(streams_of[2], 3), TOKENS // TOK_DEV)
    routes = jax.vmap(lambda own, number: assign_block(jax.random.fold_in(streams_of[2], 2), own, number, TOK_DEV, EXPERTS, TOP, CAP, 2))(routes_keys, routes_turns).reshape((TOKENS, TOP))
    gates = jnp.clip(0.1 + 0.9 * jax.random.uniform(streams_of[3], (TOKENS, TOP), jnp.float32) ** steps_of(streams_of[3], (TOKENS, TOP), ((0, 128),), -0.2, 0.2), 0.1, 1.0)
    gate_weight = normal_values(streams_of[4], (EXPERTS, LATENT, FF), LATENT ** -0.5, 0.1875, ((0, 128), (2, 4)))
    up_weight = normal_values(streams_of[5], (EXPERTS, LATENT, FF), LATENT ** -0.5, 0.1875, ((0, 128), (2, 4)))
    down_weight = normal_values(streams_of[6], (EXPERTS, FF, LATENT), FF ** -0.5, 0.15625, ((0, 128), (2, 4)))
    dec_weight = normal_values(streams_of[7], (LATENT, D), LATENT ** -0.5, 0.1875, ((0, 128), (1, 4)))
    return {"tokens": tokens, "enc_weight": enc_weight, "routes": routes, "gates": gates, "gate_weight": gate_weight, "up_weight": up_weight, "down_weight": down_weight, "dec_weight": dec_weight}


def reference(tokens, enc_weight, routes, gates, gate_weight, up_weight, down_weight, dec_weight):
    latent = jnp.dot(tokens, enc_weight, preferred_element_type=jnp.float32).astype(jnp.bfloat16)
    group_count = TOKENS // TOK_DEV
    blocked = routes.reshape(group_count, TOK_DEV * TOP)

    def ranks(chosen):
        onehot = (chosen[:, None] == jnp.arange(EXPERTS, dtype=jnp.int32)[None, :]).astype(jnp.int32)
        earlier = jnp.cumsum(onehot, axis=0) - onehot
        return jnp.sum(earlier * onehot, axis=1).astype(jnp.int32)

    position = lax.map(ranks, blocked)
    group_ids = jnp.arange(group_count, dtype=jnp.int32)[:, None]
    slot_rows = N_EXPERT * CAP
    target = (blocked * slot_rows + group_ids * CAP + position).reshape(-1).astype(jnp.int32)
    source_row = (jnp.arange(TOKENS * TOP, dtype=jnp.int32) // TOP).astype(jnp.int32)
    slots = jnp.zeros((EXPERTS * slot_rows, LATENT), jnp.bfloat16).at[target].set(latent[source_row])
    slots = slots.reshape(EXPERTS, slot_rows, LATENT)

    def expert(inputs):
        arrived, gate_matrix, up_matrix, down_matrix = inputs
        gate_part = jnp.dot(arrived, gate_matrix, preferred_element_type=jnp.float32)
        up_part = jnp.dot(arrived, up_matrix, preferred_element_type=jnp.float32)
        activation = (jax.nn.silu(gate_part) * up_part).astype(jnp.bfloat16)
        return jnp.dot(activation, down_matrix, preferred_element_type=jnp.float32).astype(jnp.bfloat16)

    answer = lax.map(expert, (slots, gate_weight, up_weight, down_weight)).reshape(EXPERTS * slot_rows, LATENT)
    picked = answer[target].astype(jnp.float32).reshape(TOKENS, TOP, LATENT)
    combined = jnp.sum(picked * gates[:, :, None], axis=1).astype(jnp.bfloat16)
    return jnp.dot(combined, dec_weight, preferred_element_type=jnp.float32).astype(jnp.bfloat16)
```

```python
import functools

import jax
import jax.numpy as jnp
from jax import lax
from jax.experimental import pallas as pl
from jax.experimental.pallas import tpu as pltpu
from jax.sharding import Mesh
from jax.sharding import PartitionSpec as P

EXPERT = ("expert_0", "expert_1", "expert_2")
BF16 = jnp.bfloat16
F32 = jnp.float32


def copy_for_each(x, axis):
    copies = jnp.broadcast_to(x, (lax.axis_size(axis), *x.shape))
    return lax.all_to_all(copies, axis, split_axis=0, concat_axis=0, tiled=True)


def gathered_rows(x):
    rows, columns = x.shape
    far = copy_for_each(x, ("expert_0", "expert_1"))
    near = copy_for_each(far, "expert_2")
    return jnp.swapaxes(near, 0, 1).reshape(-1, columns)


def ring(size, step):
    return [(i, (i + step) % size) for i in range(size)]


def packed(gate, up, down):
    gate_part = [gate[:, c : c + 128] for c in range(0, gate.shape[1], 128)]
    up_part = [up[:, c : c + 128] for c in range(0, up.shape[1], 128)]
    return jnp.concatenate(
        [*gate_part, down[:, :128], *up_part, down[:, 128:]], axis=0
    )


def expert_kernel(quarter, slots, own, left, right, over_a, over_b, out, w, act, sems):
    latent = slots.shape[1]
    hidden = act.shape[1] // 4
    half = over_a.shape[0]
    blocks = hidden // 128
    copies = []
    for i, ref in enumerate((own, left, right)):
        copies.append([pltpu.make_async_copy(ref, w.at[i], sems.at[i])])
    copies.append(
        [
            pltpu.make_async_copy(over_a, w.at[3, pl.ds(0, half)], sems.at[3]),
            pltpu.make_async_copy(over_b, w.at[3, pl.ds(half, half)], sems.at[4]),
        ]
    )
    for group in copies:
        for copy in group:
            copy.start()
    me = quarter[0]
    places = [lax.rem(me + offset, 4) for offset in (0, 3, 1, 2)]
    rows = slots[...]
    for i in range(4):
        for copy in copies[i]:
            copy.wait()
        weights = jnp.concatenate(
            [w[i, start + b * latent : start + (b + 1) * latent, :] for start in (0, half) for b in range(blocks)],
            axis=1,
        )
        both = jnp.dot(rows, weights, preferred_element_type=F32)
        gate_part, up_part = both[:, :hidden], both[:, hidden:]
        value = gate_part / (1.0 + jnp.exp(-gate_part)) * up_part
        act[:, pl.ds(pl.multiple_of(places[i] * hidden, 128), hidden)] = value.astype(BF16)
    start = blocks * latent
    for i in range(4):
        weights = jnp.concatenate([w[i, start:half, :], w[i, half + start : 2 * half, :]], axis=1)
        answer = jnp.dot(act[...], weights, preferred_element_type=F32)
        out[:, pl.ds(pl.multiple_of(places[i] * 256, 128), 256)] = answer.astype(BF16)


def experts(quarter, slots, own, left, right, over_a, over_b):
    rows, latent = slots.shape
    hidden = 1536
    any_space = pl.BlockSpec(memory_space=pl.ANY)
    vmem = pl.BlockSpec(memory_space=pltpu.VMEM)
    return pl.pallas_call(
        expert_kernel,
        out_shape=jax.ShapeDtypeStruct((rows, latent), BF16),
        in_specs=[pl.BlockSpec(memory_space=pltpu.SMEM), vmem] + [any_space] * 5,
        out_specs=vmem,
        scratch_shapes=[
            pltpu.VMEM((4, *own.shape), BF16),
            pltpu.VMEM((rows, hidden), BF16),
            pltpu.SemaphoreType.DMA((5,)),
        ],
        compiler_params=pltpu.CompilerParams(vmem_limit_bytes=40 * 2**20),
        cost_estimate=pl.CostEstimate(
            flops=2 * rows * latent * hidden * 3, bytes_accessed=12 * 2**20, transcendentals=rows * hidden
        ),
    )(quarter, slots, own, left, right, over_a, over_b)


def on_device(tokens, enc_weight, routes, gates, gate_weight, up_weight, down_weight, dec_weight):
    groups = lax.axis_size(EXPERT)
    shares = lax.axis_size("hidden")
    me = lax.axis_index("hidden").astype(jnp.int32)
    token_count, choice_count = routes.shape
    capacity = min(token_count, 2 * token_count * choice_count // groups)
    depth = capacity // shares

    own = packed(gate_weight[0], up_weight[0], down_weight[0])
    half = own.shape[0] // 2
    to_right, to_left = ring(shares, 1), ring(shares, -1)
    left = lax.ppermute(own, "hidden", to_right)
    right = lax.ppermute(own, "hidden", to_left)
    over_a = lax.ppermute(left[:half], "hidden", to_right)
    over_b = lax.ppermute(right[half:], "hidden", to_left)

    names = jnp.arange(groups, dtype=jnp.int32)[:, None, None]
    match = routes.T[None] == names
    chosen = jnp.any(match, axis=1)
    weight = jnp.sum(jnp.where(match, gates.T[None], 0.0), axis=1)
    order = jnp.arange(token_count)
    before = (order[:, None] < order[None, :]).astype(BF16)
    position = jnp.dot(chosen.astype(BF16), before, preferred_element_type=F32).astype(jnp.int32)
    place = jnp.where(chosen, position - me * depth, -1)
    picks = place[:, None, :] == jnp.arange(depth, dtype=jnp.int32)[None, :, None]
    pick = picks.astype(BF16).reshape(groups * depth, token_count)
    scale = jnp.where(picks, weight[:, None, :], 0.0).reshape(groups * depth, token_count)
    scale_high = scale.astype(BF16)
    scale_low = (scale - scale_high.astype(F32)).astype(BF16)

    latent = jnp.dot(tokens, gathered_rows(enc_weight), preferred_element_type=F32).astype(BF16)
    latent_all = jnp.swapaxes(copy_for_each(latent, "hidden"), 0, 1).reshape(token_count, -1)
    width = latent_all.shape[1]
    outgoing = jnp.dot(pick, latent_all, preferred_element_type=F32).astype(BF16)
    arrived = lax.all_to_all(
        outgoing.reshape(groups, depth, width), EXPERT, split_axis=0, concat_axis=0, tiled=True
    ).reshape(groups * depth, width)

    answer = experts(me[None], arrived, own, left, right, over_a, over_b)
    returned = lax.all_to_all(
        answer.reshape(groups, depth, width), EXPERT, split_axis=0, concat_axis=0, tiled=True
    ).reshape(groups * depth, width)

    contract = (((0,), (0,)), ((), ()))
    partial = lax.dot_general(scale_high, returned, contract, preferred_element_type=F32)
    partial = partial + lax.dot_general(scale_low, returned, contract, preferred_element_type=F32)
    sent = partial.astype(BF16)
    total = partial
    for step in (1, -1, 2):
        total = total + lax.ppermute(sent, "hidden", ring(shares, step)).astype(F32)
    combined = total.astype(BF16)
    dec = lax.all_gather(dec_weight, EXPERT, axis=0, tiled=True)
    return jnp.dot(combined, dec, preferred_element_type=F32).astype(BF16)


def solution(mesh):
    split = Mesh(
        mesh.devices.reshape(8, 8, 2, mesh.shape["hidden"]),
        ("expert_0", "expert_1", "expert_2", "hidden"),
    )
    return jax.shard_map(
        on_device,
        mesh=split,
        in_specs=(
            P(EXPERT, None),
            P(EXPERT, "hidden"),
            P(EXPERT, None),
            P(EXPERT, None),
            P(EXPERT, None, "hidden"),
            P(EXPERT, None, "hidden"),
            P(EXPERT, None, "hidden"),
            P(EXPERT, "hidden"),
        ),
        out_specs=P(EXPERT, "hidden"),
        check_vma=False,
    )
```

```python
import jax
import jax.numpy as jnp
from jax import lax
from jax.experimental import pallas as pl
from jax.experimental.pallas import tpu as pltpu
from jax.sharding import Mesh
from jax.sharding import PartitionSpec as P

FAR = ("z_far", "y_far")
CHIP = ("z_far", "z_near", "y_far", "y_near")
EXPERT = (*CHIP, "core")
BF16 = jnp.bfloat16
F32 = jnp.float32
DEPTH = 4
ANY = pl.BlockSpec(memory_space=pl.ANY)
VMEM = pl.BlockSpec(memory_space=pltpu.VMEM)
SMEM = pl.BlockSpec(memory_space=pltpu.SMEM)
PARAMS = pltpu.CompilerParams(vmem_limit_bytes=40 * 2**20)


def copy_for_each(x, axis):
    copies = jnp.broadcast_to(x, (lax.axis_size(axis), *x.shape))
    return lax.all_to_all(copies, axis, split_axis=0, concat_axis=0, tiled=True)


def ring(size, step):
    return [(i, (i + step) % size) for i in range(size)]


def message_rows(left, right):
    left, right = left.reshape(-1, 8, 128), right.reshape(-1, 8, 128)
    upper = lax.broadcasted_iota(jnp.int32, left.shape, 1) < DEPTH
    even = jnp.where(upper, left, pltpu.roll(right, DEPTH, 1))
    odd = jnp.where(upper, pltpu.roll(left, DEPTH, 1), right)
    return even, odd


def slot_rows(even, odd):
    left, right = message_rows(even, odd)
    return left.reshape(-1, 128), right.reshape(-1, 128)


def store_messages(out, blocks):
    for pair in range(2):
        done = [message_rows(b[:, :128], b[:, 128:]) for b in blocks[2 * pair : 2 * pair + 2]]
        for parity in range(2):
            rows = jnp.concatenate([done[0][parity], done[1][parity]], axis=1)
            out[:, parity, 16 * pair : 16 * pair + 16, :] = rows.astype(BF16)


def load_slots(messages, slots):
    for pair in range(2):
        even = messages[:, 0, 16 * pair : 16 * pair + 16, :].astype(F32)
        odd = messages[:, 1, 16 * pair : 16 * pair + 16, :].astype(F32)
        for half in range(2):
            rows = slice(8 * half, 8 * half + 8)
            left, right = slot_rows(even[:, rows], odd[:, rows])
            column = 512 * pair + 256 * half
            slots[:, column : column + 128] = left.astype(BF16)
            slots[:, column + 128 : column + 256] = right.astype(BF16)


def pack_kernel(gate, up, down, out):
    row = 0
    for part in (gate, up):
        for ref, columns in ((part, part.shape[1]), (down, 128)):
            first = 128 if ref is down and part is up else 0
            for c in range(first, first + columns, 128):
                out[row : row + ref.shape[0], :] = ref[:, c : c + 128]
                row += ref.shape[0]


def packed(gate, up, down):
    latent, hidden = gate.shape
    return pl.pallas_call(
        pack_kernel,
        out_shape=jax.ShapeDtypeStruct((2 * (hidden // 128) * latent + 2 * down.shape[0], 128), BF16),
        in_specs=[VMEM] * 3,
        out_specs=VMEM,
        compiler_params=PARAMS,
    )(gate, up, down)


def route_kernel(quarter, routes, gates, pick, high, low):
    choices, tokens = routes.shape
    shape = pick.shape
    row = lax.broadcasted_iota(jnp.int32, shape, 0)
    expert, slot = row // DEPTH, lax.rem(row, DEPTH)
    weight = jnp.zeros(shape, F32)
    chosen = jnp.zeros(shape, F32)
    for k in range(choices):
        match = routes[k : k + 1, :] == expert
        chosen = chosen + jnp.where(match, 1.0, 0.0)
        weight = weight + jnp.where(match, gates[k : k + 1, :], 0.0)
    earlier = lax.broadcasted_iota(jnp.int32, (tokens, tokens), 0) < lax.broadcasted_iota(
        jnp.int32, (tokens, tokens), 1
    )
    before = jnp.dot(chosen.astype(BF16), jnp.where(earlier, 1.0, 0.0).astype(BF16), preferred_element_type=F32)
    here = before == (quarter[0] * DEPTH + slot).astype(F32)
    pick[...] = jnp.where(here, chosen, 0.0).astype(BF16)
    scale = jnp.where(here, weight, 0.0)
    first = scale.astype(BF16)
    high[...] = first
    low[...] = (scale - first.astype(F32)).astype(BF16)


def route(quarter, routes, gates, groups):
    out = jax.ShapeDtypeStruct((groups * DEPTH, routes.shape[1]), BF16)
    return pl.pallas_call(
        route_kernel,
        out_shape=(out, out, out),
        in_specs=[SMEM, VMEM, VMEM],
        out_specs=(VMEM, VMEM, VMEM),
        compiler_params=PARAMS,
    )(quarter, routes, gates)


def latent_kernel(where, tokens, *refs):
    sources, (out, enc, sems) = refs[:8], refs[8:]
    z, y, core = where[0], where[1], where[2]
    copies = []
    for i, ref in enumerate(sources):
        zi = 1 - z if i & 2 else z
        yi = 1 - y if i & 1 else y
        ci = 1 - core if i & 4 else core
        for far in range(enc.shape[0]):
            copies.append(
                pltpu.make_async_copy(
                    ref.at[far, :, pl.ds(0, enc.shape[5])], enc.at[far, zi, :, yi, ci], sems.at[i, far]
                )
            )
    for copy in copies:
        copy.start()
    for copy in copies:
        copy.wait()
    weights = enc[...].reshape(tokens.shape[1], enc.shape[-1])
    latent = jnp.dot(tokens[...], weights, preferred_element_type=F32).astype(BF16)
    for i in range(out.shape[0]):
        out[i] = latent


def latent_copies(where, tokens, sources, rows, count):
    far, _, columns = sources[0].shape[1:]
    return pl.pallas_call(
        latent_kernel,
        out_shape=jax.ShapeDtypeStruct((count, tokens.shape[0], columns), BF16),
        in_specs=[SMEM, VMEM] + [ANY] * 8,
        out_specs=VMEM,
        scratch_shapes=[
            pltpu.VMEM((far, 2, far, 2, 2, rows, columns), BF16),
            pltpu.SemaphoreType.DMA((8, far)),
        ],
        compiler_params=PARAMS,
    )(where, tokens, *sources)


def dispatch_kernel(pick, latent, out):
    store_messages(
        out, [jnp.dot(pick[...], latent[i], preferred_element_type=F32) for i in range(latent.shape[0])]
    )


def dispatched(pick, latent):
    return pl.pallas_call(
        dispatch_kernel,
        out_shape=jax.ShapeDtypeStruct((pick.shape[0] // (2 * DEPTH), 2, 8 * DEPTH, 128), BF16),
        in_specs=[VMEM, VMEM],
        out_specs=VMEM,
        compiler_params=PARAMS,
    )(pick, latent)


def expert_kernel(quarter, messages, own, left, right, over_a, over_b, out, w, slots, act, sems):
    latent = slots.shape[1]
    hidden = act.shape[1] // 4
    half = over_a.shape[0]
    blocks = hidden // 128
    copies = [[pltpu.make_async_copy(ref, w.at[i], sems.at[i])] for i, ref in enumerate((own, left, right))]
    copies.append(
        [
            pltpu.make_async_copy(over_a, w.at[3, pl.ds(0, half)], sems.at[3]),
            pltpu.make_async_copy(over_b, w.at[3, pl.ds(half, half)], sems.at[4]),
        ]
    )
    for group in copies:
        for copy in group:
            copy.start()
    me = quarter[0]
    load_slots(messages, slots)
    rows = slots[...]
    for i, offset in enumerate((0, 3, 1, 2)):
        for copy in copies[i]:
            copy.wait()
        weights = jnp.concatenate(
            [w[i, start + b * latent : start + (b + 1) * latent, :] for start in (0, half) for b in range(blocks)],
            axis=1,
        )
        both = jnp.dot(rows, weights, preferred_element_type=F32)
        gate_part, up_part = both[:, :hidden], both[:, hidden:]
        value = gate_part / (1.0 + jnp.exp(-gate_part)) * up_part
        place = lax.rem(me + offset, 4)
        act[:, pl.ds(pl.multiple_of(place * hidden, 128), hidden)] = value.astype(BF16)
    start = blocks * latent
    answers = []
    for i in range(4):
        weights = jnp.concatenate([w[i, start:half, :], w[i, half + start : 2 * half, :]], axis=1)
        answers.append(jnp.dot(act[...], weights, preferred_element_type=F32))
    store_messages(out, answers)


def experts(quarter, messages, own, left, right, over_a, over_b):
    rows, latent, hidden = messages.shape[0] * 2 * DEPTH, 1024, 1536
    return pl.pallas_call(
        expert_kernel,
        out_shape=jax.ShapeDtypeStruct(messages.shape, BF16),
        in_specs=[SMEM, VMEM] + [ANY] * 5,
        out_specs=VMEM,
        scratch_shapes=[
            pltpu.VMEM((4, *own.shape), BF16),
            pltpu.VMEM((rows, latent), BF16),
            pltpu.VMEM((rows, hidden), BF16),
            pltpu.SemaphoreType.DMA((5,)),
        ],
        compiler_params=pltpu.CompilerParams(vmem_limit_bytes=60 * 2**20),
        cost_estimate=pl.CostEstimate(
            flops=2 * rows * latent * hidden * 3, bytes_accessed=12 * 2**20, transcendentals=rows * hidden
        ),
    )(quarter, messages, own, left, right, over_a, over_b)


def combine_kernel(quarter, messages, high, low, total, sent, slots):
    load_slots(messages, slots)
    contract = (((0,), (0,)), ((), ()))
    me = quarter[0]
    partial = lax.dot_general(high[...], slots[...], contract, preferred_element_type=F32)
    partial = partial + lax.dot_general(low[...], slots[...], contract, preferred_element_type=F32)
    for i, offset in enumerate((0, 3, 1, 2)):
        column = pl.multiple_of(lax.rem(me + offset, 4) * 256, 128)
        block = partial[:, 256 * i : 256 * i + 256]
        total[:, pl.ds(column, 256)] = block
        sent[:, pl.ds(column, 256)] = block.astype(BF16)


def combine(quarter, messages, high, low):
    rows, tokens = high.shape
    return pl.pallas_call(
        combine_kernel,
        out_shape=(jax.ShapeDtypeStruct((tokens, 1024), F32), jax.ShapeDtypeStruct((tokens, 1024), BF16)),
        in_specs=[SMEM, VMEM, VMEM, VMEM],
        out_specs=(VMEM, VMEM),
        scratch_shapes=[pltpu.VMEM((rows, 1024), BF16)],
        compiler_params=PARAMS,
    )(quarter, messages, high, low)


def exchanged(messages):
    flat = messages.reshape(-1, *messages.shape[2:])
    return lax.all_to_all(flat, EXPERT, split_axis=0, concat_axis=0, tiled=True).reshape(messages.shape)


def gathered(enc, dec):
    columns = enc.shape[1]
    message = jnp.concatenate([enc, *(dec[:, c : c + columns] for c in range(0, dec.shape[1], columns))], axis=0)
    far = copy_for_each(message, FAR)
    far = far.reshape(*(lax.axis_size(a) for a in FAR), *message.shape)
    swap = ring(2, 1)
    here = [
        far,
        lax.ppermute(far, "y_near", swap),
        lax.ppermute(far, "z_near", swap),
        lax.ppermute(far, ("z_near", "y_near"), [(i, 3 - i) for i in range(4)]),
    ]
    return here + [lax.ppermute(part, "core", swap) for part in here]


def placed(sources, where, start, shape):
    rows, width = shape
    far, columns = sources[0].shape[0], sources[0].shape[-1]
    whole = jnp.zeros((far, 2, far, 2, 2, rows, width), BF16)
    for i, part in enumerate(sources):
        block = part[:, :, start:].reshape(far, far, width // columns, rows, columns)
        block = jnp.swapaxes(block, 2, 3).reshape(far, 1, far, 1, 1, rows, width)
        place = [jnp.where(i & bit, 1 - where[n], where[n]) for n, bit in enumerate((2, 1, 4))]
        whole = lax.dynamic_update_slice(whole, block, (0, place[0], 0, place[1], place[2], 0, 0))
    return whole.reshape(-1, width)


def on_device(tokens, enc_weight, routes, gates, gate_weight, up_weight, down_weight, dec_weight):
    groups = lax.axis_size(EXPERT)
    shares = lax.axis_size("hidden")
    quarter = lax.axis_index("hidden").astype(jnp.int32)[None]

    own = packed(gate_weight[0], up_weight[0], down_weight[0])
    own, enc_weight = lax.optimization_barrier((own, enc_weight))
    half = own.shape[0] // 2
    to_right, to_left = ring(shares, 1), ring(shares, -1)
    left = lax.ppermute(own, "hidden", to_right)
    right = lax.ppermute(own, "hidden", to_left)

    pick, high, low = route(quarter, routes.T, gates.T, groups)
    where = jnp.stack([lax.axis_index(a).astype(jnp.int32) for a in ("z_near", "y_near", "core")])
    sources = gathered(enc_weight, dec_weight)
    latent = latent_copies(where, tokens, sources, enc_weight.shape[0], shares)
    latent, left, right, pick, high, low = lax.optimization_barrier((latent, left, right, pick, high, low))
    over_a = lax.ppermute(left[:half], "hidden", to_right)
    over_b = lax.ppermute(right[half:], "hidden", to_left)
    latent_all = lax.all_to_all(latent, "hidden", split_axis=0, concat_axis=0, tiled=True)
    arrived = exchanged(dispatched(pick, latent_all))
    dec = placed(sources, where, enc_weight.shape[0], dec_weight.shape)
    returned = exchanged(experts(quarter, arrived, own, left, right, over_a, over_b))
    total, sent = combine(quarter, returned, high, low)
    for step in (1, -1, 2):
        total = total + lax.ppermute(sent, "hidden", ring(shares, step)).astype(F32)
    return jnp.dot(total.astype(BF16), dec, preferred_element_type=F32).astype(BF16)


def solution(mesh):
    split = Mesh(
        mesh.devices.reshape(4, 2, 4, 2, 2, mesh.shape["hidden"]),
        (*EXPERT, "hidden"),
    )
    return jax.shard_map(
        on_device,
        mesh=split,
        in_specs=(
            P(EXPERT, None),
            P(EXPERT, "hidden"),
            P(EXPERT, None),
            P(EXPERT, None),
            P(EXPERT, None, "hidden"),
            P(EXPERT, None, "hidden"),
            P(EXPERT, None, "hidden"),
            P(EXPERT, "hidden"),
        ),
        out_specs=P(EXPERT, "hidden"),
        check_vma=False,
    )
```

```python
import jax
import jax.numpy as jnp
from jax import lax
from jax.experimental import pallas as pl
from jax.experimental.pallas import tpu as pltpu
from jax.sharding import Mesh
from jax.sharding import PartitionSpec as P

FAR = ("z_far", "y_far")
CHIP = ("z_far", "z_near", "y_far", "y_near")
EXPERT = (*CHIP, "core")
BF16 = jnp.bfloat16
F32 = jnp.float32
SWAP = [(0, 1), (1, 0)]
DEPTH = 4
ANY = pl.BlockSpec(memory_space=pl.ANY)
VMEM = pl.BlockSpec(memory_space=pltpu.VMEM)
SMEM = pl.BlockSpec(memory_space=pltpu.SMEM)
PARAMS = pltpu.CompilerParams(vmem_limit_bytes=40 * 2**20)


def copy_for_each(x, axis):
    copies = jnp.broadcast_to(x, (lax.axis_size(axis), *x.shape))
    return lax.all_to_all(copies, axis, split_axis=0, concat_axis=0, tiled=True)


def ring(size, step):
    return [(i, (i + step) % size) for i in range(size)]


def message_rows(left, right):
    left, right = left.reshape(-1, 8, 128), right.reshape(-1, 8, 128)
    upper = lax.broadcasted_iota(jnp.int32, left.shape, 1) < DEPTH
    even = jnp.where(upper, left, pltpu.roll(right, DEPTH, 1))
    odd = jnp.where(upper, pltpu.roll(left, DEPTH, 1), right)
    return even, odd


def slot_rows(even, odd):
    left, right = message_rows(even, odd)
    return left.reshape(-1, 128), right.reshape(-1, 128)


def store_messages(out, blocks):
    for pair in range(2):
        done = [message_rows(b[:, :128], b[:, 128:]) for b in blocks[2 * pair : 2 * pair + 2]]
        for parity in range(2):
            rows = jnp.concatenate([done[0][parity], done[1][parity]], axis=1)
            out[:, parity, 16 * pair : 16 * pair + 16, :] = rows.astype(BF16)


def load_slots(messages, slots):
    for pair in range(2):
        even = messages[:, 0, 16 * pair : 16 * pair + 16, :].astype(F32)
        odd = messages[:, 1, 16 * pair : 16 * pair + 16, :].astype(F32)
        for half in range(2):
            rows = slice(8 * half, 8 * half + 8)
            left, right = slot_rows(even[:, rows], odd[:, rows])
            column = 512 * pair + 256 * half
            slots[:, column : column + 128] = left.astype(BF16)
            slots[:, column + 128 : column + 256] = right.astype(BF16)


def pack_kernel(gate, up, down, out_a, out_b):
    for part, out, first in ((gate, out_a, 0), (up, out_b, 128)):
        row = 0
        for ref, start, stop in ((part, 0, part.shape[1]), (down, first, first + 128)):
            for c in range(start, stop, 128):
                out[row : row + ref.shape[0], :] = ref[:, c : c + 128]
                row += ref.shape[0]


def packed(gate, up, down):
    latent, hidden = gate.shape
    out = jax.ShapeDtypeStruct((hidden // 128 * latent + down.shape[0], 128), BF16)
    return pl.pallas_call(
        pack_kernel,
        out_shape=(out, out),
        in_specs=[VMEM] * 3,
        out_specs=(VMEM, VMEM),
        compiler_params=PARAMS,
    )(gate, up, down)


def route_kernel(quarter, routes, gates, pick, high, low):
    choices, tokens = routes.shape
    shape = pick.shape
    row = lax.broadcasted_iota(jnp.int32, shape, 0)
    expert, slot = row // DEPTH, lax.rem(row, DEPTH)
    weight = jnp.zeros(shape, F32)
    chosen = jnp.zeros(shape, F32)
    for k in range(choices):
        match = routes[k : k + 1, :] == expert
        chosen = chosen + jnp.where(match, 1.0, 0.0)
        weight = weight + jnp.where(match, gates[k : k + 1, :], 0.0)
    earlier = lax.broadcasted_iota(jnp.int32, (tokens, tokens), 0) < lax.broadcasted_iota(
        jnp.int32, (tokens, tokens), 1
    )
    before = jnp.dot(chosen.astype(BF16), jnp.where(earlier, 1.0, 0.0).astype(BF16), preferred_element_type=F32)
    here = before == (quarter[0] * DEPTH + slot).astype(F32)
    pick[...] = jnp.where(here, chosen, 0.0).astype(BF16)
    scale = jnp.where(here, weight, 0.0)
    first = scale.astype(BF16)
    high[...] = first
    low[...] = (scale - first.astype(F32)).astype(BF16)


def route(quarter, routes, gates, groups):
    out = jax.ShapeDtypeStruct((groups * DEPTH, routes.shape[1]), BF16)
    return pl.pallas_call(
        route_kernel,
        out_shape=(out, out, out),
        in_specs=[SMEM, VMEM, VMEM],
        out_specs=(VMEM, VMEM, VMEM),
        compiler_params=PARAMS,
    )(quarter, routes, gates)


def latent_kernel(where, tokens, *refs):
    sources, (out, enc, sems) = refs[:8], refs[8:]
    z, y, core = where[0], where[1], where[2]
    copies = []
    for i, ref in enumerate(sources):
        zi = 1 - z if i & 2 else z
        yi = 1 - y if i & 1 else y
        ci = 1 - core if i & 4 else core
        for far in range(enc.shape[0]):
            copies.append(
                pltpu.make_async_copy(
                    ref.at[far, :, pl.ds(0, enc.shape[5])], enc.at[far, zi, :, yi, ci], sems.at[i, far]
                )
            )
    for copy in copies:
        copy.start()
    for copy in copies:
        copy.wait()
    weights = enc[...].reshape(tokens.shape[1], enc.shape[-1])
    latent = jnp.dot(tokens[...], weights, preferred_element_type=F32).astype(BF16)
    for i in range(out.shape[0]):
        out[i] = latent


def latent_copies(where, tokens, sources, rows, count):
    far, _, columns = sources[0].shape[1:]
    return pl.pallas_call(
        latent_kernel,
        out_shape=jax.ShapeDtypeStruct((count, tokens.shape[0], columns), BF16),
        in_specs=[SMEM, VMEM] + [ANY] * 8,
        out_specs=VMEM,
        scratch_shapes=[
            pltpu.VMEM((far, 2, far, 2, 2, rows, columns), BF16),
            pltpu.SemaphoreType.DMA((8, far)),
        ],
        compiler_params=PARAMS,
    )(where, tokens, *sources)


def dispatch_kernel(pick, latent, out):
    store_messages(
        out, [jnp.dot(pick[...], latent[i], preferred_element_type=F32) for i in range(latent.shape[0])]
    )


def dispatched(pick, latent):
    return pl.pallas_call(
        dispatch_kernel,
        out_shape=jax.ShapeDtypeStruct((pick.shape[0] // (2 * DEPTH), 2, 8 * DEPTH, 128), BF16),
        in_specs=[VMEM, VMEM],
        out_specs=VMEM,
        compiler_params=PARAMS,
    )(pick, latent)


def expert_kernel(quarter, messages, *refs):
    weights, (out, w, slots, act, sems) = refs[:8], refs[8:]
    latent = slots.shape[1]
    hidden = act.shape[1] // 4
    blocks = hidden // 128
    copies = [pltpu.make_async_copy(ref, w.at[i // 2, i % 2], sems.at[i]) for i, ref in enumerate(weights)]
    for copy in copies:
        copy.start()
    me = quarter[0]
    load_slots(messages, slots)
    rows = slots[...]
    for i, offset in enumerate((0, 3, 1, 2)):
        copies[2 * i].wait()
        copies[2 * i + 1].wait()
        both = jnp.dot(
            rows,
            jnp.concatenate(
                [w[i, part, b * latent : (b + 1) * latent, :] for part in range(2) for b in range(blocks)], axis=1
            ),
            preferred_element_type=F32,
        )
        gate_part, up_part = both[:, :hidden], both[:, hidden:]
        value = gate_part / (1.0 + jnp.exp(-gate_part)) * up_part
        place = lax.rem(me + offset, 4)
        act[:, pl.ds(pl.multiple_of(place * hidden, 128), hidden)] = value.astype(BF16)
    answers = []
    for i in range(4):
        down = jnp.concatenate([w[i, part, blocks * latent :, :] for part in range(2)], axis=1)
        answers.append(jnp.dot(act[...], down, preferred_element_type=F32))
    store_messages(out, answers)


def experts(quarter, messages, *weights):
    rows, latent, hidden = messages.shape[0] * 2 * DEPTH, 1024, 1536
    return pl.pallas_call(
        expert_kernel,
        out_shape=jax.ShapeDtypeStruct(messages.shape, BF16),
        in_specs=[SMEM, VMEM] + [ANY] * 8,
        out_specs=VMEM,
        scratch_shapes=[
            pltpu.VMEM((4, 2, *weights[0].shape), BF16),
            pltpu.VMEM((rows, latent), BF16),
            pltpu.VMEM((rows, hidden), BF16),
            pltpu.SemaphoreType.DMA((8,)),
        ],
        compiler_params=pltpu.CompilerParams(vmem_limit_bytes=60 * 2**20),
        cost_estimate=pl.CostEstimate(
            flops=2 * rows * latent * hidden * 3, bytes_accessed=12 * 2**20, transcendentals=rows * hidden
        ),
    )(quarter, messages, *weights)


def combine_kernel(quarter, messages, high, low, total, sent, slots):
    load_slots(messages, slots)
    contract = (((0,), (0,)), ((), ()))
    me = quarter[0]
    partial = lax.dot_general(high[...], slots[...], contract, preferred_element_type=F32)
    partial = partial + lax.dot_general(low[...], slots[...], contract, preferred_element_type=F32)
    for i, offset in enumerate((0, 3, 1, 2)):
        column = pl.multiple_of(lax.rem(me + offset, 4) * 256, 128)
        block = partial[:, 256 * i : 256 * i + 256]
        total[:, pl.ds(column, 256)] = block
        sent[:, pl.ds(column, 256)] = block.astype(BF16)


def combine(quarter, messages, high, low):
    rows, tokens = high.shape
    return pl.pallas_call(
        combine_kernel,
        out_shape=(jax.ShapeDtypeStruct((tokens, 1024), F32), jax.ShapeDtypeStruct((tokens, 1024), BF16)),
        in_specs=[SMEM, VMEM, VMEM, VMEM],
        out_specs=(VMEM, VMEM),
        scratch_shapes=[pltpu.VMEM((rows, 1024), BF16)],
        compiler_params=PARAMS,
    )(quarter, messages, high, low)


def exchanged(messages):
    flat = messages.reshape(-1, *messages.shape[2:])
    return lax.all_to_all(flat, EXPERT, split_axis=0, concat_axis=0, tiled=True).reshape(messages.shape)


def from_far(enc, dec, *others):
    rows, columns = enc.shape
    message = jnp.concatenate([enc, *(dec[:, c : c + columns] for c in range(0, dec.shape[1], columns))], axis=0)
    far = copy_for_each(message, FAR).reshape(*(lax.axis_size(a) for a in FAR), *message.shape)
    far, *others = lax.optimization_barrier((far, *others))
    return far[:, :, :rows], far[:, :, rows:], *others


def beside(size, first):
    return [size - 1 - i if first and i in (0, size - 1) else i + 1 if i % 2 == first else i - 1 for i in range(size)]


def from_near(far, first):
    z, y = CHIP[:2], CHIP[2:]
    partner = beside(lax.axis_size(y), first)
    size = len(partner)
    pairs = list(enumerate(partner))
    corners = [(i, partner[i // size] * size + partner[i % size]) for i in range(size * size)]
    return [
        far,
        lax.ppermute(far, y, pairs),
        lax.ppermute(far, z, pairs),
        lax.ppermute(far, CHIP, corners),
    ]


def placed(sources, where, shape):
    rows, width = shape
    far, columns = sources[0].shape[0], sources[0].shape[-1]
    whole = jnp.zeros((far, 2, far, 2, 2, rows, width), BF16)
    for i, part in enumerate(sources):
        block = part.reshape(far, far, width // columns, rows, columns)
        block = jnp.swapaxes(block, 2, 3).reshape(far, 1, far, 1, 1, rows, width)
        place = [jnp.where(i & bit, 1 - where[n], where[n]) for n, bit in enumerate((2, 1, 4))]
        whole = lax.dynamic_update_slice(whole, block, (0, place[0], 0, place[1], place[2], 0, 0))
    return whole.reshape(-1, width)


def on_device(tokens, enc_weight, routes, gates, gate_weight, up_weight, down_weight, dec_weight):
    groups = lax.axis_size(EXPERT)
    shares = lax.axis_size("hidden")
    quarter = lax.axis_index("hidden").astype(jnp.int32)[None]

    own_a, own_b = packed(gate_weight[0], up_weight[0], down_weight[0])
    own_a, own_b, enc_weight, dec_weight = lax.optimization_barrier((own_a, own_b, enc_weight, dec_weight))
    to_right, to_left = ring(shares, 1), ring(shares, -1)
    left_a = lax.ppermute(own_a, "hidden", to_right)
    right_a = lax.ppermute(own_a, "hidden", to_left)
    left_b = lax.ppermute(own_b, "hidden", to_right)
    right_b = lax.ppermute(own_b, "hidden", to_left)

    pick, high, low = route(quarter, routes.T, gates.T, groups)
    where = jnp.stack([lax.axis_index(a).astype(jnp.int32) for a in ("z_near", "y_near", "core")])
    enc_far, dec_far, left_a, right_a = from_far(enc_weight, dec_weight, left_a, right_a)
    enc_parts = from_near(enc_far, 0)
    enc_parts = enc_parts + [lax.ppermute(part, "core", SWAP) for part in enc_parts]
    latent = latent_copies(where, tokens, enc_parts, enc_weight.shape[0], shares)
    latent, left_a, right_a, left_b, right_b, pick, high, low = lax.optimization_barrier(
        (latent, left_a, right_a, left_b, right_b, pick, high, low)
    )
    over_a = lax.ppermute(left_a, "hidden", to_right)
    over_b = lax.ppermute(right_b, "hidden", to_left)
    latent_all = lax.all_to_all(latent, "hidden", split_axis=0, concat_axis=0, tiled=True)
    arrived = exchanged(dispatched(pick, latent_all))
    dec_far, latent_all = lax.optimization_barrier((dec_far, latent_all))
    arrived, *dec_parts = lax.optimization_barrier((arrived, *from_near(dec_far, 1)))
    dec_parts = jnp.stack(dec_parts)
    dec_other = lax.ppermute(dec_parts, "core", SWAP)
    dec = placed([*dec_parts, *dec_other], where, dec_weight.shape)
    returned = exchanged(
        experts(quarter, arrived, own_a, own_b, left_a, left_b, right_a, right_b, over_a, over_b)
    )
    total, sent = combine(quarter, returned, high, low)
    for step in (1, -1, 2):
        total = total + lax.ppermute(sent, "hidden", ring(shares, step)).astype(F32)
    return jnp.dot(total.astype(BF16), dec, preferred_element_type=F32).astype(BF16)


def solution(mesh):
    split = Mesh(
        mesh.devices.reshape(4, 2, 4, 2, 2, mesh.shape["hidden"]),
        (*EXPERT, "hidden"),
    )
    return jax.shard_map(
        on_device,
        mesh=split,
        in_specs=(
            P(EXPERT, None),
            P(EXPERT, "hidden"),
            P(EXPERT, None),
            P(EXPERT, None),
            P(EXPERT, None, "hidden"),
            P(EXPERT, None, "hidden"),
            P(EXPERT, None, "hidden"),
            P(EXPERT, "hidden"),
        ),
        out_specs=P(EXPERT, "hidden"),
        check_vma=False,
    )
```

```python
import jax
import jax.numpy as jnp
from jax import lax
from jax.experimental import pallas as pl
from jax.experimental.pallas import tpu as pltpu
from jax.sharding import Mesh
from jax.sharding import PartitionSpec as P

FAR = ("z_far", "y_far")
CHIP = ("z_far", "z_near", "y_far", "y_near")
EXPERT = (*CHIP, "core")
BF16 = jnp.bfloat16
F32 = jnp.float32
SWAP = [(0, 1), (1, 0)]
DEPTH = 4
ANY = pl.BlockSpec(memory_space=pl.ANY)
VMEM = pl.BlockSpec(memory_space=pltpu.VMEM)
SMEM = pl.BlockSpec(memory_space=pltpu.SMEM)
PARAMS = pltpu.CompilerParams(vmem_limit_bytes=40 * 2**20)


def copy_for_each(x, axis):
    copies = jnp.broadcast_to(x, (lax.axis_size(axis), *x.shape))
    return lax.all_to_all(copies, axis, split_axis=0, concat_axis=0, tiled=True)


def ring(size, step):
    return [(i, (i + step) % size) for i in range(size)]


def message_rows(left, right):
    left, right = left.reshape(-1, 8, 128), right.reshape(-1, 8, 128)
    upper = lax.broadcasted_iota(jnp.int32, left.shape, 1) < DEPTH
    even = jnp.where(upper, left, pltpu.roll(right, DEPTH, 1))
    odd = jnp.where(upper, pltpu.roll(left, DEPTH, 1), right)
    return even, odd


def slot_rows(even, odd):
    left, right = message_rows(even, odd)
    return left.reshape(-1, 128), right.reshape(-1, 128)


def store_messages(out, blocks):
    for pair in range(2):
        done = [message_rows(b[:, :128], b[:, 128:]) for b in blocks[2 * pair : 2 * pair + 2]]
        for parity in range(2):
            rows = jnp.concatenate([done[0][parity], done[1][parity]], axis=1)
            out[:, parity, 16 * pair : 16 * pair + 16, :] = rows.astype(BF16)


def load_slots(messages, slots):
    for pair in range(2):
        even = messages[:, 0, 16 * pair : 16 * pair + 16, :].astype(F32)
        odd = messages[:, 1, 16 * pair : 16 * pair + 16, :].astype(F32)
        for half in range(2):
            rows = slice(8 * half, 8 * half + 8)
            left, right = slot_rows(even[:, rows], odd[:, rows])
            column = 512 * pair + 256 * half
            slots[:, column : column + 128] = left.astype(BF16)
            slots[:, column + 128 : column + 256] = right.astype(BF16)


def pack_kernel(gate, up, down, out_a, out_b, gate_in, up_in, down_in, sems):
    copies = [
        pltpu.make_async_copy(source, target, sems.at[i])
        for i, (source, target) in enumerate(((gate, gate_in), (down, down_in), (up, up_in)))
    ]
    for copy in copies:
        copy.start()
    copies[0].wait()
    copies[1].wait()
    for part, out, first in ((gate_in, out_a, 0), (up_in, out_b, 128)):
        if part is up_in:
            copies[2].wait()
        row = 0
        for ref, start, stop in ((part, 0, part.shape[1]), (down_in, first, first + 128)):
            for c in range(start, stop, 128):
                out[row : row + ref.shape[0], :] = ref[:, c : c + 128]
                row += ref.shape[0]


def packed(gate, up, down):
    latent, hidden = gate.shape
    out = jax.ShapeDtypeStruct((hidden // 128 * latent + down.shape[0], 128), BF16)
    return pl.pallas_call(
        pack_kernel,
        out_shape=(out, out),
        in_specs=[ANY] * 3,
        out_specs=(VMEM, VMEM),
        scratch_shapes=[pltpu.VMEM(x.shape, BF16) for x in (gate, up, down)] + [pltpu.SemaphoreType.DMA((3,))],
        compiler_params=pltpu.CompilerParams(vmem_limit_bytes=62 * 2**20),
    )(gate, up, down)


def route_kernel(quarter, routes, gates, pick, high, low):
    choices, tokens = routes.shape
    shape = pick.shape
    row = lax.broadcasted_iota(jnp.int32, shape, 0)
    expert, slot = row // DEPTH, lax.rem(row, DEPTH)
    weight = jnp.zeros(shape, F32)
    chosen = jnp.zeros(shape, F32)
    for k in range(choices):
        match = routes[k : k + 1, :] == expert
        chosen = chosen + jnp.where(match, 1.0, 0.0)
        weight = weight + jnp.where(match, gates[k : k + 1, :], 0.0)
    earlier = lax.broadcasted_iota(jnp.int32, (tokens, tokens), 0) < lax.broadcasted_iota(
        jnp.int32, (tokens, tokens), 1
    )
    before = jnp.dot(chosen.astype(BF16), jnp.where(earlier, 1.0, 0.0).astype(BF16), preferred_element_type=F32)
    here = before == (quarter[0] * DEPTH + slot).astype(F32)
    pick[...] = jnp.where(here, chosen, 0.0).astype(BF16)
    scale = jnp.where(here, weight, 0.0)
    first = scale.astype(BF16)
    high[...] = first
    low[...] = (scale - first.astype(F32)).astype(BF16)


def route(quarter, routes, gates, groups):
    out = jax.ShapeDtypeStruct((groups * DEPTH, routes.shape[1]), BF16)
    return pl.pallas_call(
        route_kernel,
        out_shape=(out, out, out),
        in_specs=[SMEM, VMEM, VMEM],
        out_specs=(VMEM, VMEM, VMEM),
        compiler_params=PARAMS,
    )(quarter, routes, gates)


def latent_kernel(where, tokens, *refs):
    sources, (out, enc, sems) = refs[:8], refs[8:]
    z, y, core = where[0], where[1], where[2]
    copies = []
    for i, ref in enumerate(sources):
        zi = 1 - z if i & 2 else z
        yi = 1 - y if i & 1 else y
        ci = 1 - core if i & 4 else core
        for far in range(enc.shape[0]):
            copies.append(
                pltpu.make_async_copy(
                    ref.at[far, :, pl.ds(0, enc.shape[5])], enc.at[far, zi, :, yi, ci], sems.at[i, far]
                )
            )
    for copy in copies:
        copy.start()
    for copy in copies:
        copy.wait()
    weights = enc[...].reshape(tokens.shape[1], enc.shape[-1])
    latent = jnp.dot(tokens[...], weights, preferred_element_type=F32).astype(BF16)
    for i in range(out.shape[0]):
        out[i] = latent


def latent_copies(where, tokens, sources, rows, count):
    far, _, columns = sources[0].shape[1:]
    return pl.pallas_call(
        latent_kernel,
        out_shape=jax.ShapeDtypeStruct((count, tokens.shape[0], columns), BF16),
        in_specs=[SMEM, VMEM] + [ANY] * 8,
        out_specs=VMEM,
        scratch_shapes=[
            pltpu.VMEM((far, 2, far, 2, 2, rows, columns), BF16),
            pltpu.SemaphoreType.DMA((8, far)),
        ],
        compiler_params=PARAMS,
    )(where, tokens, *sources)


def dispatch_kernel(pick, latent, out):
    store_messages(
        out, [jnp.dot(pick[...], latent[i], preferred_element_type=F32) for i in range(latent.shape[0])]
    )


def dispatched(pick, latent):
    return pl.pallas_call(
        dispatch_kernel,
        out_shape=jax.ShapeDtypeStruct((pick.shape[0] // (2 * DEPTH), 2, 8 * DEPTH, 128), BF16),
        in_specs=[VMEM, VMEM],
        out_specs=VMEM,
        compiler_params=PARAMS,
    )(pick, latent)


def expert_kernel(quarter, messages, *refs):
    weights, (out, w, slots, act, sems) = refs[:8], refs[8:]
    latent = slots.shape[1]
    hidden = act.shape[1] // 4
    blocks = hidden // 128
    copies = [pltpu.make_async_copy(ref, w.at[i // 2, i % 2], sems.at[i]) for i, ref in enumerate(weights)]
    for copy in copies[:4]:
        copy.start()
    me = quarter[0]
    load_slots(messages, slots)
    rows = slots[...]
    for i, offset in enumerate((0, 3, 1, 2)):
        copies[2 * i].wait()
        copies[2 * i + 1].wait()
        if i < 2:
            copies[2 * i + 4].start()
            copies[2 * i + 5].start()
        both = jnp.dot(
            rows,
            jnp.concatenate(
                [w[i, part, b * latent : (b + 1) * latent, :] for part in range(2) for b in range(blocks)], axis=1
            ),
            preferred_element_type=F32,
        )
        gate_part, up_part = both[:, :hidden], both[:, hidden:]
        value = gate_part / (1.0 + jnp.exp(-gate_part)) * up_part
        place = lax.rem(me + offset, 4)
        act[:, pl.ds(pl.multiple_of(place * hidden, 128), hidden)] = value.astype(BF16)
    answers = []
    for i in range(4):
        down = jnp.concatenate([w[i, part, blocks * latent :, :] for part in range(2)], axis=1)
        answers.append(jnp.dot(act[...], down, preferred_element_type=F32))
    store_messages(out, answers)


def experts(quarter, messages, *weights):
    rows, latent, hidden = messages.shape[0] * 2 * DEPTH, 1024, 1536
    return pl.pallas_call(
        expert_kernel,
        out_shape=jax.ShapeDtypeStruct(messages.shape, BF16),
        in_specs=[SMEM, VMEM] + [ANY] * 8,
        out_specs=VMEM,
        scratch_shapes=[
            pltpu.VMEM((4, 2, *weights[0].shape), BF16),
            pltpu.VMEM((rows, latent), BF16),
            pltpu.VMEM((rows, hidden), BF16),
            pltpu.SemaphoreType.DMA((8,)),
        ],
        compiler_params=pltpu.CompilerParams(vmem_limit_bytes=60 * 2**20),
        cost_estimate=pl.CostEstimate(
            flops=2 * rows * latent * hidden * 3, bytes_accessed=12 * 2**20, transcendentals=rows * hidden
        ),
    )(quarter, messages, *weights)


def combine_kernel(quarter, messages, high, low, total, sent, slots):
    load_slots(messages, slots)
    contract = (((0,), (0,)), ((), ()))
    me = quarter[0]
    partial = lax.dot_general(high[...], slots[...], contract, preferred_element_type=F32)
    partial = partial + lax.dot_general(low[...], slots[...], contract, preferred_element_type=F32)
    for i, offset in enumerate((0, 3, 1, 2)):
        column = pl.multiple_of(lax.rem(me + offset, 4) * 256, 128)
        block = partial[:, 256 * i : 256 * i + 256]
        total[:, pl.ds(column, 256)] = block
        sent[:, pl.ds(column, 256)] = block.astype(BF16)


def combine(quarter, messages, high, low):
    rows, tokens = high.shape
    return pl.pallas_call(
        combine_kernel,
        out_shape=(jax.ShapeDtypeStruct((tokens, 1024), F32), jax.ShapeDtypeStruct((tokens, 1024), BF16)),
        in_specs=[SMEM, VMEM, VMEM, VMEM],
        out_specs=(VMEM, VMEM),
        scratch_shapes=[pltpu.VMEM((rows, 1024), BF16)],
        compiler_params=PARAMS,
    )(quarter, messages, high, low)


def exchanged(messages):
    flat = messages.reshape(-1, *messages.shape[2:])
    return lax.all_to_all(flat, EXPERT, split_axis=0, concat_axis=0, tiled=True).reshape(messages.shape)


def from_far(enc, dec, *others):
    rows, columns = enc.shape
    message = jnp.concatenate([enc, *(dec[:, c : c + columns] for c in range(0, dec.shape[1], columns))], axis=0)
    far = copy_for_each(message, FAR).reshape(*(lax.axis_size(a) for a in FAR), *message.shape)
    far, *others = lax.optimization_barrier((far, *others))
    return far[:, :, :rows], far[:, :, rows:], *others


def beside(size, first):
    return [size - 1 - i if first and i in (0, size - 1) else i + 1 if i % 2 == first else i - 1 for i in range(size)]


def from_near(far, first):
    z, y = CHIP[:2], CHIP[2:]
    partner = beside(lax.axis_size(y), first)
    size = len(partner)
    pairs = list(enumerate(partner))
    corners = [(i, partner[i // size] * size + partner[i % size]) for i in range(size * size)]
    return [
        far,
        lax.ppermute(far, y, pairs),
        lax.ppermute(far, z, pairs),
        lax.ppermute(far, CHIP, corners),
    ]


def placed(sources, where, shape):
    rows, width = shape
    far, columns = sources[0].shape[0], sources[0].shape[-1]
    whole = jnp.zeros((far, 2, far, 2, 2, rows, width), BF16)
    for i, part in enumerate(sources):
        block = part.reshape(far, far, width // columns, rows, columns)
        block = jnp.swapaxes(block, 2, 3).reshape(far, 1, far, 1, 1, rows, width)
        place = [jnp.where(i & bit, 1 - where[n], where[n]) for n, bit in enumerate((2, 1, 4))]
        whole = lax.dynamic_update_slice(whole, block, (0, place[0], 0, place[1], place[2], 0, 0))
    return whole.reshape(-1, width)


def on_device(tokens, enc_weight, routes, gates, gate_weight, up_weight, down_weight, dec_weight):
    groups = lax.axis_size(EXPERT)
    shares = lax.axis_size("hidden")
    quarter = lax.axis_index("hidden").astype(jnp.int32)[None]

    own_a, own_b = packed(gate_weight[0], up_weight[0], down_weight[0])
    own_a, own_b, enc_weight, dec_weight = lax.optimization_barrier((own_a, own_b, enc_weight, dec_weight))
    to_right, to_left = ring(shares, 1), ring(shares, -1)
    left_a = lax.ppermute(own_a, "hidden", to_right)
    right_a = lax.ppermute(own_a, "hidden", to_left)
    left_b = lax.ppermute(own_b, "hidden", to_right)
    right_b = lax.ppermute(own_b, "hidden", to_left)

    pick, high, low = route(quarter, routes.T, gates.T, groups)
    where = jnp.stack([lax.axis_index(a).astype(jnp.int32) for a in ("z_near", "y_near", "core")])
    enc_far, dec_far, left_a, right_a = from_far(enc_weight, dec_weight, left_a, right_a)
    enc_parts = from_near(enc_far, 0)
    enc_parts = enc_parts + [lax.ppermute(part, "core", SWAP) for part in enc_parts]
    latent = latent_copies(where, tokens, enc_parts, enc_weight.shape[0], shares)
    latent, left_a, right_a, left_b, right_b, pick, high, low = lax.optimization_barrier(
        (latent, left_a, right_a, left_b, right_b, pick, high, low)
    )
    over_a = lax.ppermute(left_a, "hidden", to_right)
    over_b = lax.ppermute(right_b, "hidden", to_left)
    latent_all = lax.all_to_all(latent, "hidden", split_axis=0, concat_axis=0, tiled=True)
    arrived = exchanged(dispatched(pick, latent_all))
    dec_far, latent_all = lax.optimization_barrier((dec_far, latent_all))
    dec_parts = from_near(dec_far, 1)
    answer = experts(quarter, arrived, own_a, own_b, left_a, left_b, right_a, right_b, over_a, over_b)
    answer, *dec_parts = lax.optimization_barrier((answer, *dec_parts))
    dec_parts = jnp.stack(dec_parts)
    dec_other = lax.ppermute(dec_parts, "core", SWAP)
    dec = placed([*dec_parts, *dec_other], where, dec_weight.shape)
    returned = exchanged(answer)
    total, sent = combine(quarter, returned, high, low)
    for step in (1, -1, 2):
        total = total + lax.ppermute(sent, "hidden", ring(shares, step)).astype(F32)
    return jnp.dot(total.astype(BF16), dec, preferred_element_type=F32).astype(BF16)


def solution(mesh):
    split = Mesh(
        mesh.devices.reshape(4, 2, 4, 2, 2, mesh.shape["hidden"]),
        (*EXPERT, "hidden"),
    )
    return jax.shard_map(
        on_device,
        mesh=split,
        in_specs=(
            P(EXPERT, None),
            P(EXPERT, "hidden"),
            P(EXPERT, None),
            P(EXPERT, None),
            P(EXPERT, None, "hidden"),
            P(EXPERT, None, "hidden"),
            P(EXPERT, None, "hidden"),
            P(EXPERT, "hidden"),
        ),
        out_specs=P(EXPERT, "hidden"),
        check_vma=False,
    )
```

```python
import jax
import jax.numpy as jnp
from jax import lax
from jax.experimental import pallas as pl
from jax.experimental.pallas import tpu as pltpu
from jax.sharding import Mesh
from jax.sharding import PartitionSpec as P

FAR = ("z_far", "y_far")
CHIP = ("z_far", "z_near", "y_far", "y_near")
EXPERT = (*CHIP, "core")
BF16 = jnp.bfloat16
F32 = jnp.float32
SWAP = [(0, 1), (1, 0)]
DEPTH = 4
ANY = pl.BlockSpec(memory_space=pl.ANY)
VMEM = pl.BlockSpec(memory_space=pltpu.VMEM)
SMEM = pl.BlockSpec(memory_space=pltpu.SMEM)
PARAMS = pltpu.CompilerParams(vmem_limit_bytes=40 * 2**20)


def copy_for_each(x, axis):
    copies = jnp.broadcast_to(x, (lax.axis_size(axis), *x.shape))
    return lax.all_to_all(copies, axis, split_axis=0, concat_axis=0, tiled=True)


def ring(size, step):
    return [(i, (i + step) % size) for i in range(size)]


def message_rows(left, right):
    left, right = left.reshape(-1, 8, 128), right.reshape(-1, 8, 128)
    upper = lax.broadcasted_iota(jnp.int32, left.shape, 1) < DEPTH
    even = jnp.where(upper, left, pltpu.roll(right, DEPTH, 1))
    odd = jnp.where(upper, pltpu.roll(left, DEPTH, 1), right)
    return even, odd


def slot_rows(even, odd):
    left, right = message_rows(even, odd)
    return left.reshape(-1, 128), right.reshape(-1, 128)


def store_messages(out, blocks):
    for pair in range(2):
        done = [message_rows(b[:, :128], b[:, 128:]) for b in blocks[2 * pair : 2 * pair + 2]]
        for parity in range(2):
            rows = jnp.concatenate([done[0][parity], done[1][parity]], axis=1)
            out[:, parity, 16 * pair : 16 * pair + 16, :] = rows.astype(BF16)


def load_slots(messages, slots):
    for pair in range(2):
        even = messages[:, 0, 16 * pair : 16 * pair + 16, :].astype(F32)
        odd = messages[:, 1, 16 * pair : 16 * pair + 16, :].astype(F32)
        for half in range(2):
            rows = slice(8 * half, 8 * half + 8)
            left, right = slot_rows(even[:, rows], odd[:, rows])
            column = 512 * pair + 256 * half
            slots[:, column : column + 128] = left.astype(BF16)
            slots[:, column + 128 : column + 256] = right.astype(BF16)


def pack_kernel(gate, up, down, out_a, out_b, gate_in, up_in, down_in, sems):
    copies = [
        pltpu.make_async_copy(source, target, sems.at[i])
        for i, (source, target) in enumerate(((gate, gate_in), (down, down_in), (up, up_in)))
    ]
    for copy in copies:
        copy.start()
    copies[0].wait()
    copies[1].wait()
    for part, out, first in ((gate_in, out_a, 0), (up_in, out_b, 128)):
        if part is up_in:
            copies[2].wait()
        row = 0
        for ref, start, stop in ((part, 0, part.shape[1]), (down_in, first, first + 128)):
            for c in range(start, stop, 128):
                out[row : row + ref.shape[0], :] = ref[:, c : c + 128]
                row += ref.shape[0]


def packed(gate, up, down):
    latent, hidden = gate.shape
    out = jax.ShapeDtypeStruct((hidden // 128 * latent + down.shape[0], 128), BF16)
    return pl.pallas_call(
        pack_kernel,
        out_shape=(out, out),
        in_specs=[ANY] * 3,
        out_specs=(VMEM, VMEM),
        scratch_shapes=[pltpu.VMEM(x.shape, BF16) for x in (gate, up, down)] + [pltpu.SemaphoreType.DMA((3,))],
        compiler_params=pltpu.CompilerParams(vmem_limit_bytes=62 * 2**20),
    )(gate, up, down)


def route_kernel(quarter, routes, gates, pick, high, low):
    choices, tokens = routes.shape
    shape = pick.shape
    row = lax.broadcasted_iota(jnp.int32, shape, 0)
    expert, slot = row // DEPTH, lax.rem(row, DEPTH)
    weight = jnp.zeros(shape, F32)
    chosen = jnp.zeros(shape, F32)
    for k in range(choices):
        match = routes[k : k + 1, :] == expert
        chosen = chosen + jnp.where(match, 1.0, 0.0)
        weight = weight + jnp.where(match, gates[k : k + 1, :], 0.0)
    earlier = lax.broadcasted_iota(jnp.int32, (tokens, tokens), 0) < lax.broadcasted_iota(
        jnp.int32, (tokens, tokens), 1
    )
    before = jnp.dot(chosen.astype(BF16), jnp.where(earlier, 1.0, 0.0).astype(BF16), preferred_element_type=F32)
    here = before == (quarter[0] * DEPTH + slot).astype(F32)
    pick[...] = jnp.where(here, chosen, 0.0).astype(BF16)
    scale = jnp.where(here, weight, 0.0)
    first = scale.astype(BF16)
    high[...] = first
    low[...] = (scale - first.astype(F32)).astype(BF16)


def route(quarter, routes, gates, groups):
    out = jax.ShapeDtypeStruct((groups * DEPTH, routes.shape[1]), BF16)
    return pl.pallas_call(
        route_kernel,
        out_shape=(out, out, out),
        in_specs=[SMEM, VMEM, VMEM],
        out_specs=(VMEM, VMEM, VMEM),
        compiler_params=PARAMS,
    )(quarter, routes, gates)


def latent_kernel(where, tokens, others, *refs):
    sources, (mine, sent, enc, sems) = refs[:4], refs[4:]
    z, y, core = where[0], where[1], where[2]
    copies = []
    for i, ref in enumerate(sources):
        zi = 1 - z if i & 2 else z
        yi = 1 - y if i & 1 else y
        for far in range(enc.shape[0]):
            copies.append(pltpu.make_async_copy(ref.at[far], enc.at[far, zi, :, yi, core], sems.at[i, far]))
    enc[:, :, :, :, 1 - core] = jnp.zeros((*enc.shape[:4], *enc.shape[5:]), BF16)
    for copy in copies:
        copy.start()
    for copy in copies:
        copy.wait()
    weights = enc[...].reshape(tokens.shape[1], enc.shape[-1])
    mine[...] = jnp.dot(tokens[...], weights, preferred_element_type=F32)
    sent[...] = jnp.dot(others[...], weights, preferred_element_type=F32)


def latent_parts(where, tokens, others, sources):
    far, _, rows, columns = sources[0].shape
    out = jax.ShapeDtypeStruct((tokens.shape[0], columns), F32)
    return pl.pallas_call(
        latent_kernel,
        out_shape=(out, out),
        in_specs=[SMEM, VMEM, VMEM] + [ANY] * 4,
        out_specs=(VMEM, VMEM),
        scratch_shapes=[
            pltpu.VMEM((far, 2, far, 2, 2, rows, columns), BF16),
            pltpu.SemaphoreType.DMA((4, far)),
        ],
        compiler_params=PARAMS,
    )(where, tokens, others, *sources)


def dispatch_kernel(pick, latent, out):
    store_messages(
        out, [jnp.dot(pick[...], latent[i], preferred_element_type=F32) for i in range(latent.shape[0])]
    )


def dispatched(pick, latent):
    return pl.pallas_call(
        dispatch_kernel,
        out_shape=jax.ShapeDtypeStruct((pick.shape[0] // (2 * DEPTH), 2, 8 * DEPTH, 128), BF16),
        in_specs=[VMEM, VMEM],
        out_specs=VMEM,
        compiler_params=PARAMS,
    )(pick, latent)


def expert_kernel(quarter, messages, *refs):
    weights, (out, w, slots, act, sems) = refs[:8], refs[8:]
    latent = slots.shape[1]
    hidden = act.shape[1] // 4
    blocks = hidden // 128
    parts = sems.shape[1]
    depth = weights[0].shape[0] // parts
    copies = []
    for i, ref in enumerate(weights):
        for j in range(parts):
            place = pl.ds(j * depth, depth)
            copies.append(pltpu.make_async_copy(ref.at[place], w.at[i // 2, i % 2, place], sems.at[i, j]))
    for copy in copies:
        copy.start()
    me = quarter[0]
    load_slots(messages, slots)
    rows = slots[...]
    for i, offset in enumerate((0, 3, 1, 2)):
        for copy in copies[2 * parts * i : 2 * parts * (i + 1)]:
            copy.wait()
        both = jnp.dot(
            rows,
            jnp.concatenate(
                [w[i, part, b * latent : (b + 1) * latent, :] for part in range(2) for b in range(blocks)], axis=1
            ),
            preferred_element_type=F32,
        )
        gate_part, up_part = both[:, :hidden], both[:, hidden:]
        value = gate_part / (1.0 + jnp.exp(-gate_part)) * up_part
        place = lax.rem(me + offset, 4)
        act[:, pl.ds(pl.multiple_of(place * hidden, 128), hidden)] = value.astype(BF16)
    answers = []
    for i in range(4):
        down = jnp.concatenate([w[i, part, blocks * latent :, :] for part in range(2)], axis=1)
        answers.append(jnp.dot(act[...], down, preferred_element_type=F32))
    store_messages(out, answers)


def experts(quarter, messages, *weights):
    rows, latent, hidden = messages.shape[0] * 2 * DEPTH, 1024, 1536
    return pl.pallas_call(
        expert_kernel,
        out_shape=jax.ShapeDtypeStruct(messages.shape, BF16),
        in_specs=[SMEM, VMEM] + [ANY] * 8,
        out_specs=VMEM,
        scratch_shapes=[
            pltpu.VMEM((4, 2, *weights[0].shape), BF16),
            pltpu.VMEM((rows, latent), BF16),
            pltpu.VMEM((rows, hidden), BF16),
            pltpu.SemaphoreType.DMA((8, 4)),
        ],
        compiler_params=pltpu.CompilerParams(vmem_limit_bytes=60 * 2**20),
        cost_estimate=pl.CostEstimate(
            flops=2 * rows * latent * hidden * 3, bytes_accessed=12 * 2**20, transcendentals=rows * hidden
        ),
    )(quarter, messages, *weights)


def combine_kernel(quarter, messages, high, low, total, sent, slots):
    load_slots(messages, slots)
    contract = (((0,), (0,)), ((), ()))
    me = quarter[0]
    partial = lax.dot_general(high[...], slots[...], contract, preferred_element_type=F32)
    partial = partial + lax.dot_general(low[...], slots[...], contract, preferred_element_type=F32)
    for i, offset in enumerate((0, 3, 1, 2)):
        column = pl.multiple_of(lax.rem(me + offset, 4) * 256, 128)
        block = partial[:, 256 * i : 256 * i + 256]
        total[:, pl.ds(column, 256)] = block
        sent[:, pl.ds(column, 256)] = block.astype(BF16)


def combine(quarter, messages, high, low):
    rows, tokens = high.shape
    return pl.pallas_call(
        combine_kernel,
        out_shape=(jax.ShapeDtypeStruct((tokens, 1024), F32), jax.ShapeDtypeStruct((tokens, 1024), BF16)),
        in_specs=[SMEM, VMEM, VMEM, VMEM],
        out_specs=(VMEM, VMEM),
        scratch_shapes=[pltpu.VMEM((rows, 1024), BF16)],
        compiler_params=PARAMS,
    )(quarter, messages, high, low)


def exchanged(messages):
    flat = messages.reshape(-1, *messages.shape[2:])
    return lax.all_to_all(flat, EXPERT, split_axis=0, concat_axis=0, tiled=True).reshape(messages.shape)


def from_far(enc, dec, *others):
    rows, columns = enc.shape
    message = jnp.concatenate([enc, *(dec[:, c : c + columns] for c in range(0, dec.shape[1], columns))], axis=0)
    far = copy_for_each(message, FAR).reshape(*(lax.axis_size(a) for a in FAR), *message.shape)
    far, *others = lax.optimization_barrier((far, *others))
    return far[:, :, :rows], far[:, :, rows:], *others


def beside(size, first):
    return [size - 1 - i if first and i in (0, size - 1) else i + 1 if i % 2 == first else i - 1 for i in range(size)]


def from_near(far, first):
    z, y = CHIP[:2], CHIP[2:]
    partner = beside(lax.axis_size(y), first)
    size = len(partner)
    pairs = list(enumerate(partner))
    corners = [(i, partner[i // size] * size + partner[i % size]) for i in range(size * size)]
    return [
        far,
        lax.ppermute(far, y, pairs),
        lax.ppermute(far, z, pairs),
        lax.ppermute(far, CHIP, corners),
    ]


def placed(sources, where, shape):
    rows, width = shape
    far, columns = sources[0].shape[0], sources[0].shape[-1]
    whole = jnp.zeros((far, 2, far, 2, 2, rows, width), BF16)
    for i, part in enumerate(sources):
        block = part.reshape(far, far, width // columns, rows, columns)
        block = jnp.swapaxes(block, 2, 3).reshape(far, 1, far, 1, 1, rows, width)
        place = [jnp.where(i & bit, 1 - where[n], where[n]) for n, bit in enumerate((2, 1, 4))]
        whole = lax.dynamic_update_slice(whole, block, (0, place[0], 0, place[1], place[2], 0, 0))
    return whole.reshape(-1, width)


def on_device(tokens, enc_weight, routes, gates, gate_weight, up_weight, down_weight, dec_weight):
    groups = lax.axis_size(EXPERT)
    shares = lax.axis_size("hidden")
    quarter = lax.axis_index("hidden").astype(jnp.int32)[None]

    own_a, own_b = packed(gate_weight[0], up_weight[0], down_weight[0])
    own_a, own_b, enc_weight, dec_weight = lax.optimization_barrier((own_a, own_b, enc_weight, dec_weight))
    to_right, to_left = ring(shares, 1), ring(shares, -1)
    left_a = lax.ppermute(own_a, "hidden", to_right)
    right_a = lax.ppermute(own_a, "hidden", to_left)
    left_b = lax.ppermute(own_b, "hidden", to_right)
    right_b = lax.ppermute(own_b, "hidden", to_left)

    pick, high, low = route(quarter, routes.T, gates.T, groups)
    where = jnp.stack([lax.axis_index(a).astype(jnp.int32) for a in ("z_near", "y_near", "core")])
    enc_far, dec_far, left_a, right_a = from_far(enc_weight, dec_weight, left_a, right_a)
    enc_parts = from_near(enc_far, 0)
    mine, sent = latent_parts(where, tokens, lax.ppermute(tokens, "core", SWAP), enc_parts)
    latent = (mine + lax.ppermute(sent, "core", SWAP)).astype(BF16)
    latent = jnp.broadcast_to(latent, (shares, *latent.shape))
    latent, left_a, right_a, left_b, right_b, pick, high, low = lax.optimization_barrier(
        (latent, left_a, right_a, left_b, right_b, pick, high, low)
    )
    over_a = lax.ppermute(left_a, "hidden", to_right)
    over_b = lax.ppermute(right_b, "hidden", to_left)
    latent_all = lax.all_to_all(latent, "hidden", split_axis=0, concat_axis=0, tiled=True)
    arrived = exchanged(dispatched(pick, latent_all))
    dec_far, latent_all = lax.optimization_barrier((dec_far, latent_all))
    dec_parts = from_near(dec_far, 1)
    answer = experts(quarter, arrived, own_a, own_b, left_a, left_b, right_a, right_b, over_a, over_b)
    answer, *dec_parts = lax.optimization_barrier((answer, *dec_parts))
    dec_parts = jnp.stack(dec_parts)
    dec_other = lax.ppermute(dec_parts, "core", SWAP)
    dec = placed([*dec_parts, *dec_other], where, dec_weight.shape)
    returned = exchanged(answer)
    total, sent = combine(quarter, returned, high, low)
    for step in (1, -1, 2):
        total = total + lax.ppermute(sent, "hidden", ring(shares, step)).astype(F32)
    return jnp.dot(total.astype(BF16), dec, preferred_element_type=F32).astype(BF16)


def solution(mesh):
    split = Mesh(
        mesh.devices.reshape(4, 2, 4, 2, 2, mesh.shape["hidden"]),
        (*EXPERT, "hidden"),
    )
    return jax.shard_map(
        on_device,
        mesh=split,
        in_specs=(
            P(EXPERT, None),
            P(EXPERT, "hidden"),
            P(EXPERT, None),
            P(EXPERT, None),
            P(EXPERT, None, "hidden"),
            P(EXPERT, None, "hidden"),
            P(EXPERT, None, "hidden"),
            P(EXPERT, "hidden"),
        ),
        out_specs=P(EXPERT, "hidden"),
        check_vma=False,
    )
```

```python
import jax
import jax.numpy as jnp
from jax import lax
from jax.experimental import pallas as pl
from jax.experimental.pallas import tpu as pltpu
from jax.sharding import Mesh
from jax.sharding import PartitionSpec as P

FAR = ("z_far", "y_far")
CHIP = ("z_far", "z_near", "y_far", "y_near")
EXPERT = (*CHIP, "core")
BF16 = jnp.bfloat16
F32 = jnp.float32
SWAP = [(0, 1), (1, 0)]
DEPTH = 4
ANY = pl.BlockSpec(memory_space=pl.ANY)
VMEM = pl.BlockSpec(memory_space=pltpu.VMEM)
SMEM = pl.BlockSpec(memory_space=pltpu.SMEM)
PARAMS = pltpu.CompilerParams(vmem_limit_bytes=40 * 2**20)


def copy_for_each(x, axis):
    copies = jnp.broadcast_to(x, (lax.axis_size(axis), *x.shape))
    return lax.all_to_all(copies, axis, split_axis=0, concat_axis=0, tiled=True)


def ring(size, step):
    return [(i, (i + step) % size) for i in range(size)]


def message_rows(left, right):
    left, right = left.reshape(-1, 8, 128), right.reshape(-1, 8, 128)
    upper = lax.broadcasted_iota(jnp.int32, left.shape, 1) < DEPTH
    even = jnp.where(upper, left, pltpu.roll(right, DEPTH, 1))
    odd = jnp.where(upper, pltpu.roll(left, DEPTH, 1), right)
    return even, odd


def slot_rows(even, odd):
    left, right = message_rows(even, odd)
    return left.reshape(-1, 128), right.reshape(-1, 128)


def store_messages(out, blocks):
    for pair in range(2):
        done = [message_rows(b[:, :128], b[:, 128:]) for b in blocks[2 * pair : 2 * pair + 2]]
        for parity in range(2):
            rows = jnp.concatenate([done[0][parity], done[1][parity]], axis=1)
            out[:, parity, 16 * pair : 16 * pair + 16, :] = rows.astype(BF16)


def load_slots(messages, slots):
    for pair in range(2):
        even = messages[:, 0, 16 * pair : 16 * pair + 16, :].astype(F32)
        odd = messages[:, 1, 16 * pair : 16 * pair + 16, :].astype(F32)
        for half in range(2):
            rows = slice(8 * half, 8 * half + 8)
            left, right = slot_rows(even[:, rows], odd[:, rows])
            column = 512 * pair + 256 * half
            slots[:, column : column + 128] = left.astype(BF16)
            slots[:, column + 128 : column + 256] = right.astype(BF16)


def pack_kernel(gate, up, down, out_a, out_b, gate_in, up_in, down_in, sems):
    copies = [
        pltpu.make_async_copy(source, target, sems.at[i])
        for i, (source, target) in enumerate(((gate, gate_in), (down, down_in), (up, up_in)))
    ]
    for copy in copies:
        copy.start()
    copies[0].wait()
    copies[1].wait()
    for part, out, first in ((gate_in, out_a, 0), (up_in, out_b, 128)):
        if part is up_in:
            copies[2].wait()
        row = 0
        for ref, start, stop in ((part, 0, part.shape[1]), (down_in, first, first + 128)):
            for c in range(start, stop, 128):
                out[row : row + ref.shape[0], :] = ref[:, c : c + 128]
                row += ref.shape[0]


def packed(gate, up, down):
    latent, hidden = gate.shape
    out = jax.ShapeDtypeStruct((hidden // 128 * latent + down.shape[0], 128), BF16)
    return pl.pallas_call(
        pack_kernel,
        out_shape=(out, out),
        in_specs=[ANY] * 3,
        out_specs=(VMEM, VMEM),
        scratch_shapes=[pltpu.VMEM(x.shape, BF16) for x in (gate, up, down)] + [pltpu.SemaphoreType.DMA((3,))],
        compiler_params=pltpu.CompilerParams(vmem_limit_bytes=62 * 2**20),
    )(gate, up, down)


def route_kernel(quarter, routes, gates, pick, high, low):
    choices, tokens = routes.shape
    shape = pick.shape
    row = lax.broadcasted_iota(jnp.int32, shape, 0)
    expert, slot = row // DEPTH, lax.rem(row, DEPTH)
    weight = jnp.zeros(shape, F32)
    chosen = jnp.zeros(shape, F32)
    for k in range(choices):
        match = routes[k : k + 1, :] == expert
        chosen = chosen + jnp.where(match, 1.0, 0.0)
        weight = weight + jnp.where(match, gates[k : k + 1, :], 0.0)
    earlier = lax.broadcasted_iota(jnp.int32, (tokens, tokens), 0) < lax.broadcasted_iota(
        jnp.int32, (tokens, tokens), 1
    )
    before = jnp.dot(chosen.astype(BF16), jnp.where(earlier, 1.0, 0.0).astype(BF16), preferred_element_type=F32)
    here = before == (quarter[0] * DEPTH + slot).astype(F32)
    pick[...] = jnp.where(here, chosen, 0.0).astype(BF16)
    scale = jnp.where(here, weight, 0.0)
    first = scale.astype(BF16)
    high[...] = first
    low[...] = (scale - first.astype(F32)).astype(BF16)


def route(quarter, routes, gates, groups):
    out = jax.ShapeDtypeStruct((groups * DEPTH, routes.shape[1]), BF16)
    return pl.pallas_call(
        route_kernel,
        out_shape=(out, out, out),
        in_specs=[SMEM, VMEM, VMEM],
        out_specs=(VMEM, VMEM, VMEM),
        compiler_params=PARAMS,
    )(quarter, routes, gates)


def latent_kernel(where, tokens, others, *refs):
    sources, (mine, sent, enc, sems) = refs[:4], refs[4:]
    z, y, core = where[0], where[1], where[2]
    copies = []
    for i, ref in enumerate(sources):
        zi = 1 - z if i & 2 else z
        yi = 1 - y if i & 1 else y
        for far in range(enc.shape[0]):
            copies.append(pltpu.make_async_copy(ref.at[far], enc.at[far, zi, :, yi, core], sems.at[i, far]))
    enc[:, :, :, :, 1 - core] = jnp.zeros((*enc.shape[:4], *enc.shape[5:]), BF16)
    for copy in copies:
        copy.start()
    for copy in copies:
        copy.wait()
    weights = enc[...].reshape(tokens.shape[1], enc.shape[-1])
    mine[...] = jnp.dot(tokens[...], weights, preferred_element_type=F32)
    sent[...] = jnp.dot(others[...], weights, preferred_element_type=F32)


def latent_parts(where, tokens, others, sources):
    far, _, rows, columns = sources[0].shape
    out = jax.ShapeDtypeStruct((tokens.shape[0], columns), F32)
    return pl.pallas_call(
        latent_kernel,
        out_shape=(out, out),
        in_specs=[SMEM, VMEM, VMEM] + [ANY] * 4,
        out_specs=(VMEM, VMEM),
        scratch_shapes=[
            pltpu.VMEM((far, 2, far, 2, 2, rows, columns), BF16),
            pltpu.SemaphoreType.DMA((4, far)),
        ],
        compiler_params=PARAMS,
    )(where, tokens, others, *sources)


def dispatch_kernel(pick, latent, out):
    store_messages(
        out, [jnp.dot(pick[...], latent[i], preferred_element_type=F32) for i in range(latent.shape[0])]
    )


def dispatched(pick, latent):
    return pl.pallas_call(
        dispatch_kernel,
        out_shape=jax.ShapeDtypeStruct((pick.shape[0] // (2 * DEPTH), 2, 8 * DEPTH, 128), BF16),
        in_specs=[VMEM, VMEM],
        out_specs=VMEM,
        compiler_params=PARAMS,
    )(pick, latent)


def fetched(pairs, sems):
    copies = [pltpu.make_async_copy(source, target, sems.at[i]) for i, (source, target) in enumerate(pairs)]
    for copy in copies:
        copy.start()
    return copies


def hidden_units(slots, w, i, blocks, latent):
    weights = jnp.concatenate(
        [w[i, part, b * latent : (b + 1) * latent, :] for part in range(2) for b in range(blocks)], axis=1
    )
    both = jnp.dot(slots, weights, preferred_element_type=F32)
    gate_part, up_part = both[:, : blocks * 128], both[:, blocks * 128 :]
    return (gate_part / (1.0 + jnp.exp(-gate_part)) * up_part).astype(BF16)


def place_of(me, i, width):
    return pl.ds(pl.multiple_of(lax.rem(me + (0, 3, 1, 2)[i], 4) * width, 128), width)


def first_kernel(quarter, messages, *refs):
    weights, (slots, act, w, sems) = refs[:6], refs[6:]
    latent, hidden = slots.shape[1], act.shape[1] // 4
    blocks = hidden // 128
    pairs = []
    for i, ref in enumerate(weights):
        for b in range(blocks):
            rows = pl.ds(b * latent, latent)
            pairs.append((ref.at[rows], w.at[i // 2, i % 2, rows]))
    copies = fetched(pairs, sems)
    load_slots(messages, slots)
    for i in range(3):
        for copy in copies[2 * blocks * i : 2 * blocks * (i + 1)]:
            copy.wait()
        act[:, place_of(quarter[0], i, hidden)] = hidden_units(slots[...], w, i, blocks, latent)


def second_kernel(quarter, slots, first, *refs):
    weights, (out, w, down, act, sems) = refs[:8], refs[8:]
    latent, hidden = slots.shape[1], act.shape[1] // 4
    blocks = hidden // 128
    pairs = []
    for i, ref in enumerate(weights[6:]):
        for b in range(blocks):
            rows = pl.ds(b * latent, latent)
            pairs.append((ref.at[rows], w.at[0, i, rows]))
    for i, ref in enumerate(weights):
        pairs.append((ref.at[pl.ds(blocks * latent, act.shape[1])], down.at[i // 2, i % 2]))
    copies = fetched(pairs, sems)
    act[...] = first[...]
    for copy in copies[: 2 * blocks]:
        copy.wait()
    act[:, place_of(quarter[0], 3, hidden)] = hidden_units(slots[...], w, 0, blocks, latent)
    answers = []
    for i in range(4):
        for copy in copies[2 * (blocks + i) : 2 * (blocks + i + 1)]:
            copy.wait()
        answers.append(
            jnp.dot(act[...], jnp.concatenate([down[i, 0], down[i, 1]], axis=1), preferred_element_type=F32)
        )
    store_messages(out, answers)


def experts(quarter, messages, *weights):
    rows, latent, hidden = messages.shape[0] * 2 * DEPTH, 1024, 1536
    gate_rows = 3 * latent
    params = pltpu.CompilerParams(vmem_limit_bytes=60 * 2**20)
    slots, act = pl.pallas_call(
        first_kernel,
        out_shape=(jax.ShapeDtypeStruct((rows, latent), BF16), jax.ShapeDtypeStruct((rows, hidden), BF16)),
        in_specs=[SMEM, VMEM] + [ANY] * 6,
        out_specs=(VMEM, VMEM),
        scratch_shapes=[pltpu.VMEM((3, 2, gate_rows, 128), BF16), pltpu.SemaphoreType.DMA((18,))],
        compiler_params=params,
        cost_estimate=pl.CostEstimate(
            flops=3 * rows * latent * hidden, bytes_accessed=6 * 2**20, transcendentals=rows * hidden
        ),
    )(quarter, messages, *weights[:6])
    return pl.pallas_call(
        second_kernel,
        out_shape=jax.ShapeDtypeStruct(messages.shape, BF16),
        in_specs=[SMEM, VMEM, VMEM] + [ANY] * 8,
        out_specs=VMEM,
        scratch_shapes=[
            pltpu.VMEM((1, 2, gate_rows, 128), BF16),
            pltpu.VMEM((4, 2, hidden, 128), BF16),
            pltpu.VMEM((rows, hidden), BF16),
            pltpu.SemaphoreType.DMA((14,)),
        ],
        compiler_params=params,
        cost_estimate=pl.CostEstimate(
            flops=3 * rows * latent * hidden, bytes_accessed=7 * 2**20, transcendentals=rows * hidden
        ),
    )(quarter, slots, act, *weights)


def combine_kernel(quarter, messages, high, low, total, sent, slots):
    load_slots(messages, slots)
    contract = (((0,), (0,)), ((), ()))
    me = quarter[0]
    partial = lax.dot_general(high[...], slots[...], contract, preferred_element_type=F32)
    partial = partial + lax.dot_general(low[...], slots[...], contract, preferred_element_type=F32)
    for i, offset in enumerate((0, 3, 1, 2)):
        column = pl.multiple_of(lax.rem(me + offset, 4) * 256, 128)
        block = partial[:, 256 * i : 256 * i + 256]
        total[:, pl.ds(column, 256)] = block
        sent[:, pl.ds(column, 256)] = block.astype(BF16)


def combine(quarter, messages, high, low):
    rows, tokens = high.shape
    return pl.pallas_call(
        combine_kernel,
        out_shape=(jax.ShapeDtypeStruct((tokens, 1024), F32), jax.ShapeDtypeStruct((tokens, 1024), BF16)),
        in_specs=[SMEM, VMEM, VMEM, VMEM],
        out_specs=(VMEM, VMEM),
        scratch_shapes=[pltpu.VMEM((rows, 1024), BF16)],
        compiler_params=PARAMS,
    )(quarter, messages, high, low)


def exchanged(messages):
    flat = messages.reshape(-1, *messages.shape[2:])
    return lax.all_to_all(flat, EXPERT, split_axis=0, concat_axis=0, tiled=True).reshape(messages.shape)


def from_far(enc, dec, *others):
    rows, columns = enc.shape
    message = jnp.concatenate([enc, *(dec[:, c : c + columns] for c in range(0, dec.shape[1], columns))], axis=0)
    far = copy_for_each(message, FAR).reshape(*(lax.axis_size(a) for a in FAR), *message.shape)
    far, *others = lax.optimization_barrier((far, *others))
    return far[:, :, :rows], far[:, :, rows:], *others


def beside(size, first):
    return [size - 1 - i if first and i in (0, size - 1) else i + 1 if i % 2 == first else i - 1 for i in range(size)]


def from_near(far, first):
    z, y = CHIP[:2], CHIP[2:]
    partner = beside(lax.axis_size(y), first)
    size = len(partner)
    pairs = list(enumerate(partner))
    corners = [(i, partner[i // size] * size + partner[i % size]) for i in range(size * size)]
    return [
        far,
        lax.ppermute(far, y, pairs),
        lax.ppermute(far, z, pairs),
        lax.ppermute(far, CHIP, corners),
    ]


def placed(sources, where, shape):
    rows, width = shape
    far, columns = sources[0].shape[0], sources[0].shape[-1]
    whole = jnp.zeros((far, 2, far, 2, 2, rows, width), BF16)
    for i, part in enumerate(sources):
        block = part.reshape(far, far, width // columns, rows, columns)
        block = jnp.swapaxes(block, 2, 3).reshape(far, 1, far, 1, 1, rows, width)
        place = [jnp.where(i & bit, 1 - where[n], where[n]) for n, bit in enumerate((2, 1, 4))]
        whole = lax.dynamic_update_slice(whole, block, (0, place[0], 0, place[1], place[2], 0, 0))
    return whole.reshape(-1, width)


def on_device(tokens, enc_weight, routes, gates, gate_weight, up_weight, down_weight, dec_weight):
    groups = lax.axis_size(EXPERT)
    shares = lax.axis_size("hidden")
    quarter = lax.axis_index("hidden").astype(jnp.int32)[None]

    own_a, own_b = packed(gate_weight[0], up_weight[0], down_weight[0])
    own_a, own_b, enc_weight, dec_weight = lax.optimization_barrier((own_a, own_b, enc_weight, dec_weight))
    to_right, to_left = ring(shares, 1), ring(shares, -1)
    left_a = lax.ppermute(own_a, "hidden", to_right)
    right_a = lax.ppermute(own_a, "hidden", to_left)
    left_b = lax.ppermute(own_b, "hidden", to_right)
    right_b = lax.ppermute(own_b, "hidden", to_left)

    pick, high, low = route(quarter, routes.T, gates.T, groups)
    where = jnp.stack([lax.axis_index(a).astype(jnp.int32) for a in ("z_near", "y_near", "core")])
    enc_far, dec_far, left_a, right_a = from_far(enc_weight, dec_weight, left_a, right_a)
    enc_parts = from_near(enc_far, 0)
    mine, sent = latent_parts(where, tokens, lax.ppermute(tokens, "core", SWAP), enc_parts)
    latent = (mine + lax.ppermute(sent, "core", SWAP)).astype(BF16)
    latent = jnp.broadcast_to(latent, (shares, *latent.shape))
    latent, left_a, right_a, left_b, right_b, pick, high, low = lax.optimization_barrier(
        (latent, left_a, right_a, left_b, right_b, pick, high, low)
    )
    over_a = lax.ppermute(left_a, "hidden", to_right)
    over_b = lax.ppermute(right_b, "hidden", to_left)
    latent_all = lax.all_to_all(latent, "hidden", split_axis=0, concat_axis=0, tiled=True)
    arrived = exchanged(dispatched(pick, latent_all))
    dec_far, latent_all = lax.optimization_barrier((dec_far, latent_all))
    dec_parts = from_near(dec_far, 1)
    answer = experts(quarter, arrived, own_a, own_b, left_a, left_b, right_a, right_b, over_a, over_b)
    answer, *dec_parts = lax.optimization_barrier((answer, *dec_parts))
    dec_parts = jnp.stack(dec_parts)
    dec_other = lax.ppermute(dec_parts, "core", SWAP)
    dec = placed([*dec_parts, *dec_other], where, dec_weight.shape)
    returned = exchanged(answer)
    total, sent = combine(quarter, returned, high, low)
    for step in (1, -1, 2):
        total = total + lax.ppermute(sent, "hidden", ring(shares, step)).astype(F32)
    return jnp.dot(total.astype(BF16), dec, preferred_element_type=F32).astype(BF16)


def solution(mesh):
    split = Mesh(
        mesh.devices.reshape(4, 2, 4, 2, 2, mesh.shape["hidden"]),
        (*EXPERT, "hidden"),
    )
    return jax.shard_map(
        on_device,
        mesh=split,
        in_specs=(
            P(EXPERT, None),
            P(EXPERT, "hidden"),
            P(EXPERT, None),
            P(EXPERT, None),
            P(EXPERT, None, "hidden"),
            P(EXPERT, None, "hidden"),
            P(EXPERT, None, "hidden"),
            P(EXPERT, "hidden"),
        ),
        out_specs=P(EXPERT, "hidden"),
        check_vma=False,
    )
```

```python
import jax
import jax.numpy as jnp
from jax import lax
from jax.experimental import pallas as pl
from jax.experimental.pallas import tpu as pltpu
from jax.sharding import Mesh
from jax.sharding import PartitionSpec as P

FAR = ("z_far", "y_far")
CHIP = ("z_far", "z_near", "y_far", "y_near")
EXPERT = (*CHIP, "core")
BF16 = jnp.bfloat16
F32 = jnp.float32
SWAP = [(0, 1), (1, 0)]
DEPTH = 4
ANY = pl.BlockSpec(memory_space=pl.ANY)
VMEM = pl.BlockSpec(memory_space=pltpu.VMEM)
SMEM = pl.BlockSpec(memory_space=pltpu.SMEM)
PARAMS = pltpu.CompilerParams(vmem_limit_bytes=40 * 2**20)


def copy_for_each(x, axis):
    copies = jnp.broadcast_to(x, (lax.axis_size(axis), *x.shape))
    return lax.all_to_all(copies, axis, split_axis=0, concat_axis=0, tiled=True)


def ring(size, step):
    return [(i, (i + step) % size) for i in range(size)]


def message_rows(left, right):
    left, right = left.reshape(-1, 8, 128), right.reshape(-1, 8, 128)
    upper = lax.broadcasted_iota(jnp.int32, left.shape, 1) < DEPTH
    even = jnp.where(upper, left, pltpu.roll(right, DEPTH, 1))
    odd = jnp.where(upper, pltpu.roll(left, DEPTH, 1), right)
    return even, odd


def slot_rows(even, odd):
    left, right = message_rows(even, odd)
    return left.reshape(-1, 128), right.reshape(-1, 128)


def store_messages(out, blocks):
    for pair in range(2):
        done = [message_rows(b[:, :128], b[:, 128:]) for b in blocks[2 * pair : 2 * pair + 2]]
        for parity in range(2):
            rows = jnp.concatenate([done[0][parity], done[1][parity]], axis=1)
            out[:, parity, 16 * pair : 16 * pair + 16, :] = rows.astype(BF16)


def load_slots(messages, slots):
    for pair in range(2):
        even = messages[:, 0, 16 * pair : 16 * pair + 16, :].astype(F32)
        odd = messages[:, 1, 16 * pair : 16 * pair + 16, :].astype(F32)
        for half in range(2):
            rows = slice(8 * half, 8 * half + 8)
            left, right = slot_rows(even[:, rows], odd[:, rows])
            column = 512 * pair + 256 * half
            slots[:, column : column + 128] = left.astype(BF16)
            slots[:, column + 128 : column + 256] = right.astype(BF16)


def pack_kernel(gate, up, down, out_a, out_b, gate_in, up_in, down_in, sems):
    copies = [
        pltpu.make_async_copy(source, target, sems.at[i])
        for i, (source, target) in enumerate(((gate, gate_in), (down, down_in), (up, up_in)))
    ]
    for copy in copies:
        copy.start()
    copies[0].wait()
    copies[1].wait()
    for part, out, first in ((gate_in, out_a, 0), (up_in, out_b, 128)):
        if part is up_in:
            copies[2].wait()
        row = 0
        for ref, start, stop in ((part, 0, part.shape[1]), (down_in, first, first + 128)):
            for c in range(start, stop, 128):
                out[row : row + ref.shape[0], :] = ref[:, c : c + 128]
                row += ref.shape[0]


def packed(gate, up, down):
    latent, hidden = gate.shape
    out = jax.ShapeDtypeStruct((hidden // 128 * latent + down.shape[0], 128), BF16)
    return pl.pallas_call(
        pack_kernel,
        out_shape=(out, out),
        in_specs=[ANY] * 3,
        out_specs=(VMEM, VMEM),
        scratch_shapes=[pltpu.VMEM(x.shape, BF16) for x in (gate, up, down)] + [pltpu.SemaphoreType.DMA((3,))],
        compiler_params=pltpu.CompilerParams(vmem_limit_bytes=62 * 2**20),
    )(gate, up, down)


def route_kernel(quarter, routes, gates, pick, high, low):
    choices, tokens = routes.shape
    shape = pick.shape
    row = lax.broadcasted_iota(jnp.int32, shape, 0)
    expert, slot = row // DEPTH, lax.rem(row, DEPTH)
    weight = jnp.zeros(shape, F32)
    chosen = jnp.zeros(shape, F32)
    for k in range(choices):
        match = routes[k : k + 1, :] == expert
        chosen = chosen + jnp.where(match, 1.0, 0.0)
        weight = weight + jnp.where(match, gates[k : k + 1, :], 0.0)
    earlier = lax.broadcasted_iota(jnp.int32, (tokens, tokens), 0) < lax.broadcasted_iota(
        jnp.int32, (tokens, tokens), 1
    )
    before = jnp.dot(chosen.astype(BF16), jnp.where(earlier, 1.0, 0.0).astype(BF16), preferred_element_type=F32)
    here = before == (quarter[0] * DEPTH + slot).astype(F32)
    pick[...] = jnp.where(here, chosen, 0.0).astype(BF16)
    scale = jnp.where(here, weight, 0.0)
    first = scale.astype(BF16)
    high[...] = first
    low[...] = (scale - first.astype(F32)).astype(BF16)


def route(quarter, routes, gates, groups):
    out = jax.ShapeDtypeStruct((groups * DEPTH, routes.shape[1]), BF16)
    return pl.pallas_call(
        route_kernel,
        out_shape=(out, out, out),
        in_specs=[SMEM, VMEM, VMEM],
        out_specs=(VMEM, VMEM, VMEM),
        compiler_params=PARAMS,
    )(quarter, routes, gates)


def latent_kernel(where, tokens, others, *refs):
    sources, (mine, sent, enc, sems) = refs[:4], refs[4:]
    z, y, core = where[0], where[1], where[2]
    copies = []
    for i, ref in enumerate(sources):
        zi = 1 - z if i & 2 else z
        yi = 1 - y if i & 1 else y
        for far in range(enc.shape[0]):
            copies.append(pltpu.make_async_copy(ref.at[far], enc.at[far, zi, :, yi, core], sems.at[i, far]))
    enc[:, :, :, :, 1 - core] = jnp.zeros((*enc.shape[:4], *enc.shape[5:]), BF16)
    for copy in copies:
        copy.start()
    for copy in copies:
        copy.wait()
    weights = enc[...].reshape(tokens.shape[1], enc.shape[-1])
    mine[...] = jnp.dot(tokens[...], weights, preferred_element_type=F32)
    sent[...] = jnp.dot(others[...], weights, preferred_element_type=F32)


def latent_parts(where, tokens, others, sources):
    far, _, rows, columns = sources[0].shape
    out = jax.ShapeDtypeStruct((tokens.shape[0], columns), F32)
    return pl.pallas_call(
        latent_kernel,
        out_shape=(out, out),
        in_specs=[SMEM, VMEM, VMEM] + [ANY] * 4,
        out_specs=(VMEM, VMEM),
        scratch_shapes=[
            pltpu.VMEM((far, 2, far, 2, 2, rows, columns), BF16),
            pltpu.SemaphoreType.DMA((4, far)),
        ],
        compiler_params=PARAMS,
    )(where, tokens, others, *sources)


def dispatch_kernel(pick, latent, out):
    store_messages(
        out, [jnp.dot(pick[...], latent[i], preferred_element_type=F32) for i in range(latent.shape[0])]
    )


def dispatched(pick, latent):
    return pl.pallas_call(
        dispatch_kernel,
        out_shape=jax.ShapeDtypeStruct((pick.shape[0] // (2 * DEPTH), 2, 8 * DEPTH, 128), BF16),
        in_specs=[VMEM, VMEM],
        out_specs=VMEM,
        compiler_params=PARAMS,
    )(pick, latent)


def fetched(pairs, sems):
    copies = [pltpu.make_async_copy(source, target, sems.at[i]) for i, (source, target) in enumerate(pairs)]
    for copy in copies:
        copy.start()
    return copies


def hidden_units(slots, w, i, blocks, latent):
    weights = jnp.concatenate(
        [w[i, part, b * latent : (b + 1) * latent, :] for part in range(2) for b in range(blocks)], axis=1
    )
    both = jnp.dot(slots, weights, preferred_element_type=F32)
    gate_part, up_part = both[:, : blocks * 128], both[:, blocks * 128 :]
    return (gate_part / (1.0 + jnp.exp(-gate_part)) * up_part).astype(BF16)


def place_of(me, i, width):
    return pl.ds(pl.multiple_of(lax.rem(me + (0, 3, 1, 2)[i], 4) * width, 128), width)


def first_kernel(quarter, messages, *refs):
    weights, (slots, act, w, sems) = refs[:6], refs[6:]
    latent, hidden = slots.shape[1], act.shape[1] // 4
    blocks = hidden // 128
    pairs = []
    for i, ref in enumerate(weights):
        for b in range(blocks):
            rows = pl.ds(b * latent, latent)
            pairs.append((ref.at[rows], w.at[i // 2, i % 2, rows]))
    copies = fetched(pairs, sems)
    load_slots(messages, slots)
    for i in range(3):
        for copy in copies[2 * blocks * i : 2 * blocks * (i + 1)]:
            copy.wait()
        act[:, place_of(quarter[0], i, hidden)] = hidden_units(slots[...], w, i, blocks, latent)


def second_kernel(quarter, slots, first, *refs):
    weights, (out, w, down, act, sems) = refs[:8], refs[8:]
    latent, hidden = slots.shape[1], act.shape[1] // 4
    blocks = hidden // 128
    pairs = []
    for i, ref in enumerate(weights[6:]):
        for b in range(blocks):
            rows = pl.ds(b * latent, latent)
            pairs.append((ref.at[rows], w.at[0, i, rows]))
    for i, ref in enumerate(weights):
        pairs.append((ref.at[pl.ds(blocks * latent, act.shape[1])], down.at[i // 2, i % 2]))
    copies = fetched(pairs, sems)
    act[...] = first[...]
    for copy in copies[: 2 * blocks]:
        copy.wait()
    act[:, place_of(quarter[0], 3, hidden)] = hidden_units(slots[...], w, 0, blocks, latent)
    answers = []
    for i in range(4):
        for copy in copies[2 * (blocks + i) : 2 * (blocks + i + 1)]:
            copy.wait()
        answers.append(
            jnp.dot(act[...], jnp.concatenate([down[i, 0], down[i, 1]], axis=1), preferred_element_type=F32)
        )
    store_messages(out, answers)


def experts(quarter, messages, *weights):
    rows, latent, hidden = messages.shape[0] * 2 * DEPTH, 1024, 1536
    gate_rows = 3 * latent
    params = pltpu.CompilerParams(vmem_limit_bytes=50 * 2**20)
    slots, act = pl.pallas_call(
        first_kernel,
        out_shape=(jax.ShapeDtypeStruct((rows, latent), BF16), jax.ShapeDtypeStruct((rows, hidden), BF16)),
        in_specs=[SMEM, VMEM] + [ANY] * 6,
        out_specs=(VMEM, VMEM),
        scratch_shapes=[pltpu.VMEM((3, 2, gate_rows, 128), BF16), pltpu.SemaphoreType.DMA((18,))],
        compiler_params=params,
        cost_estimate=pl.CostEstimate(
            flops=3 * rows * latent * hidden, bytes_accessed=6 * 2**20, transcendentals=rows * hidden
        ),
    )(quarter, messages, *weights[:6])
    return pl.pallas_call(
        second_kernel,
        out_shape=jax.ShapeDtypeStruct(messages.shape, BF16),
        in_specs=[SMEM, VMEM, VMEM] + [ANY] * 8,
        out_specs=VMEM,
        scratch_shapes=[
            pltpu.VMEM((1, 2, gate_rows, 128), BF16),
            pltpu.VMEM((4, 2, hidden, 128), BF16),
            pltpu.VMEM((rows, hidden), BF16),
            pltpu.SemaphoreType.DMA((14,)),
        ],
        compiler_params=params,
        cost_estimate=pl.CostEstimate(
            flops=3 * rows * latent * hidden, bytes_accessed=7 * 2**20, transcendentals=rows * hidden
        ),
    )(quarter, slots, act, *weights)


def combine_kernel(quarter, messages, high, low, total, sent, slots):
    load_slots(messages, slots)
    contract = (((0,), (0,)), ((), ()))
    me = quarter[0]
    partial = lax.dot_general(high[...], slots[...], contract, preferred_element_type=F32)
    partial = partial + lax.dot_general(low[...], slots[...], contract, preferred_element_type=F32)
    for i, offset in enumerate((0, 3, 1, 2)):
        column = pl.multiple_of(lax.rem(me + offset, 4) * 256, 128)
        block = partial[:, 256 * i : 256 * i + 256]
        total[:, pl.ds(column, 256)] = block
        sent[:, pl.ds(column, 256)] = block.astype(BF16)


def combine(quarter, messages, high, low):
    rows, tokens = high.shape
    return pl.pallas_call(
        combine_kernel,
        out_shape=(jax.ShapeDtypeStruct((tokens, 1024), F32), jax.ShapeDtypeStruct((tokens, 1024), BF16)),
        in_specs=[SMEM, VMEM, VMEM, VMEM],
        out_specs=(VMEM, VMEM),
        scratch_shapes=[pltpu.VMEM((rows, 1024), BF16)],
        compiler_params=PARAMS,
    )(quarter, messages, high, low)


def exchanged(messages):
    flat = messages.reshape(-1, *messages.shape[2:])
    return lax.all_to_all(flat, EXPERT, split_axis=0, concat_axis=0, tiled=True).reshape(messages.shape)


def from_far(enc, dec, *others):
    rows, columns = enc.shape
    message = jnp.concatenate([enc, *(dec[:, c : c + columns] for c in range(0, dec.shape[1], columns))], axis=0)
    far = copy_for_each(message, FAR).reshape(*(lax.axis_size(a) for a in FAR), *message.shape)
    far, *others = lax.optimization_barrier((far, *others))
    return far[:, :, :rows], far[:, :, rows:], *others


def beside(size, first):
    return [size - 1 - i if first and i in (0, size - 1) else i + 1 if i % 2 == first else i - 1 for i in range(size)]


def from_near(far, first):
    z, y = CHIP[:2], CHIP[2:]
    partner = beside(lax.axis_size(y), first)
    size = len(partner)
    pairs = list(enumerate(partner))
    corners = [(i, partner[i // size] * size + partner[i % size]) for i in range(size * size)]
    return [
        far,
        lax.ppermute(far, y, pairs),
        lax.ppermute(far, z, pairs),
        lax.ppermute(far, CHIP, corners),
    ]


def placed(sources, where, shape):
    rows, width = shape
    far, columns = sources[0].shape[0], sources[0].shape[-1]
    whole = jnp.zeros((far, 2, far, 2, 2, rows, width), BF16)
    for i, part in enumerate(sources):
        block = part.reshape(far, far, width // columns, rows, columns)
        block = jnp.swapaxes(block, 2, 3).reshape(far, 1, far, 1, 1, rows, width)
        place = [jnp.where(i & bit, 1 - where[n], where[n]) for n, bit in enumerate((2, 1, 4))]
        whole = lax.dynamic_update_slice(whole, block, (0, place[0], 0, place[1], place[2], 0, 0))
    return whole.reshape(-1, width)


def on_device(tokens, enc_weight, routes, gates, gate_weight, up_weight, down_weight, dec_weight):
    groups = lax.axis_size(EXPERT)
    shares = lax.axis_size("hidden")
    quarter = lax.axis_index("hidden").astype(jnp.int32)[None]

    own_a, own_b = packed(gate_weight[0], up_weight[0], down_weight[0])
    own_a, own_b, enc_weight, dec_weight = lax.optimization_barrier((own_a, own_b, enc_weight, dec_weight))
    to_right, to_left = ring(shares, 1), ring(shares, -1)
    left_a = lax.ppermute(own_a, "hidden", to_right)
    right_a = lax.ppermute(own_a, "hidden", to_left)
    left_b = lax.ppermute(own_b, "hidden", to_right)
    right_b = lax.ppermute(own_b, "hidden", to_left)

    pick, high, low = route(quarter, routes.T, gates.T, groups)
    where = jnp.stack([lax.axis_index(a).astype(jnp.int32) for a in ("z_near", "y_near", "core")])
    enc_far, dec_far, left_a, right_a = from_far(enc_weight, dec_weight, left_a, right_a)
    enc_parts = from_near(enc_far, 0)
    mine, sent = latent_parts(where, tokens, lax.ppermute(tokens, "core", SWAP), enc_parts)
    latent = (mine + lax.ppermute(sent, "core", SWAP)).astype(BF16)
    latent = jnp.broadcast_to(latent, (shares, *latent.shape))
    latent, left_a, right_a, left_b, right_b, pick, high, low = lax.optimization_barrier(
        (latent, left_a, right_a, left_b, right_b, pick, high, low)
    )
    over_a = lax.ppermute(left_a, "hidden", to_right)
    over_b = lax.ppermute(right_b, "hidden", to_left)
    latent_all = lax.all_to_all(latent, "hidden", split_axis=0, concat_axis=0, tiled=True)
    arrived = exchanged(dispatched(pick, latent_all))
    dec_far, latent_all = lax.optimization_barrier((dec_far, latent_all))
    dec_parts = from_near(dec_far, 1)
    answer = experts(quarter, arrived, own_a, own_b, left_a, left_b, right_a, right_b, over_a, over_b)
    answer, *dec_parts = lax.optimization_barrier((answer, *dec_parts))
    dec_parts = jnp.stack(dec_parts)
    dec_other = lax.ppermute(dec_parts, "core", SWAP)
    dec = placed([*dec_parts, *dec_other], where, dec_weight.shape)
    returned = exchanged(answer)
    total, sent = combine(quarter, returned, high, low)
    for step in (1, -1, 2):
        total = total + lax.ppermute(sent, "hidden", ring(shares, step)).astype(F32)
    return jnp.dot(total.astype(BF16), dec, preferred_element_type=F32).astype(BF16)


def solution(mesh):
    split = Mesh(
        mesh.devices.reshape(4, 2, 4, 2, 2, mesh.shape["hidden"]),
        (*EXPERT, "hidden"),
    )
    return jax.shard_map(
        on_device,
        mesh=split,
        in_specs=(
            P(EXPERT, None),
            P(EXPERT, "hidden"),
            P(EXPERT, None),
            P(EXPERT, None),
            P(EXPERT, None, "hidden"),
            P(EXPERT, None, "hidden"),
            P(EXPERT, None, "hidden"),
            P(EXPERT, "hidden"),
        ),
        out_specs=P(EXPERT, "hidden"),
        check_vma=False,
    )
```
